512 devices in a mesh: seq: 64 (over y_lo, z, core), head: 8 (over x, y_hi).
Axes of the slice: x: 4, y: 4 (y_hi: 2, y_lo: 2; y = y_hi * 2 + y_lo), z: 16, core: 2. Of those that a mesh axis runs over, the one named last changes fastest.
Arguments:
- query_main: bfloat16 [8192, 2048], P(('seq', 'head')), may hold values from -5 to 5
- key_main: bfloat16 [8192, 2048], P(('seq', 'head')), may hold values from -5 to 5
- value_main: bfloat16 [8192, 2048], P(('seq', 'head')), may hold values from -5 to 5
- query_tan: bfloat16 [8192, 2048], P(('seq', 'head')), may hold values from -5 to 5
- key_tan: bfloat16 [8192, 2048], P(('seq', 'head')), may hold values from -5 to 5
- value_tan: bfloat16 [8192, 2048], P(('seq', 'head')), may hold values from -5 to 5
- positions: int32 [8192], P(('seq', 'head')), may hold values from 0 to 1073741823, as said below
Outputs:
- attended: bfloat16 [8192, 2048], P(('seq', 'head'))
- attended_tan: bfloat16 [8192, 2048], P(('seq', 'head'))
The draws below stay inside these ranges and needn't reach their ends.
Inputs may be any that keep to these rules, and one draw needn't show every extreme that they name: `positions`: 8192 distinct values.
All inputs are finite; a program needn't handle non-finite values.
Results may differ from the reference program's by a relative error of at most 0.035.
Values may be sent and summed in bfloat16 or wider, within the bound.
A program may use at most 128 MiB of HBM per device.

```python
import math
import jax
import jax.numpy as jnp
from jax import lax

HEADS = 16
HEAD_DIM = 128
SEQ = 8192


def draw_query_main(key, part):
    own = jax.random.fold_in(key, 1)
    values = jnp.clip(jax.random.normal(own, (SEQ, HEADS * HEAD_DIM), jnp.float32), -4.0, 4.0)
    return values.astype(jnp.bfloat16)


def draw_key_main(key, part):
    own = jax.random.fold_in(key, 2)
    values = jnp.clip(jax.random.normal(own, (SEQ, HEADS * HEAD_DIM), jnp.float32), -4.0, 4.0)
    return values.astype(jnp.bfloat16)


def draw_positions(key, part):
    key = jax.random.fold_in(key, 3)
    first, second = jax.random.split(key)
    top_value = 2 ** 30 - SEQ
    raw = jax.random.randint(first, (SEQ,), 0, top_value, dtype=jnp.int32)
    ranked = jnp.sort(raw)
    ranked = ranked.at[0].set(0).at[SEQ - 1].set(top_value)
    keyed = ranked + jnp.arange(SEQ, dtype=jnp.int32)
    order = jax.random.permutation(second, SEQ).astype(jnp.int32)
    return keyed[order].astype(jnp.int32)


def block_levels(rng, dims, shards, smallest, high):
    level, own = 1.0, jax.random.fold_in(rng, 6)
    for axis_at, parts in shards:
        steps = jnp.exp(jax.random.uniform(jax.random.fold_in(own, axis_at), (parts,), jnp.float32, smallest / len(shards), high / len(shards)))
        level = level * jnp.repeat(steps, dims[axis_at] // parts).reshape([-1 if axis == axis_at else 1 for axis in range(len(dims))])
    return level


def normal_values(rng, extent, scale, bound, cuts=(), kind=jnp.bfloat16):
    drawn = jax.random.normal(rng, extent, jnp.float32) * scale
    if len(cuts) > 0:
        drawn = block_levels(rng, extent, cuts, -0.22, 0.18) * drawn
    return jnp.clip(drawn, min=-bound, max=bound).astype(kind)


def setup_inputs(seed: int = 0) -> dict:
    streams_of = jax.random.split(jax.random.key(seed), 8)
    query_main = draw_query_main(jax.random.fold_in(streams_of[7], 71), 0)
    key_main = draw_key_main(jax.random.fold_in(streams_of[7], 71), 0)
    value_main = normal_values(streams_of[2], (SEQ, HEADS * HEAD_DIM), 1.0, 5.0, ((0, 512),))
    query_tan = normal_values(streams_of[3], (SEQ, HEADS * HEAD_DIM), 1.0, 5.0, ((0, 512),))
    key_tan = normal_values(streams_of[4], (SEQ, HEADS * HEAD_DIM), 1.0, 5.0, ((0, 512),))
    value_tan = normal_values(streams_of[5], (SEQ, HEADS * HEAD_DIM), 1.0, 5.0, ((0, 512),))
    positions = draw_positions(jax.random.fold_in(streams_of[7], 71), 0)
    return {"query_main": query_main, "key_main": key_main, "value_main": value_main, "query_tan": query_tan, "key_tan": key_tan, "value_tan": value_tan, "positions": positions}


def reference(query_main, key_main, value_main, query_tan, key_tan, value_tan, positions):
    scale = HEAD_DIM ** -0.5
    rows = math.gcd(SEQ, 256)
    queries = query_main.reshape(SEQ, HEADS, HEAD_DIM).astype(jnp.float32)
    keys = key_main.reshape(SEQ, HEADS, HEAD_DIM).astype(jnp.float32)
    values = value_main.reshape(SEQ, HEADS, HEAD_DIM).astype(jnp.float32)
    query_dot = query_tan.reshape(SEQ, HEADS, HEAD_DIM).astype(jnp.float32)
    key_dot = key_tan.reshape(SEQ, HEADS, HEAD_DIM).astype(jnp.float32)
    value_dot = value_tan.reshape(SEQ, HEADS, HEAD_DIM).astype(jnp.float32)

    def one_block(start):
        block_q = lax.dynamic_slice_in_dim(queries, start, rows, 0)
        block_dq = lax.dynamic_slice_in_dim(query_dot, start, rows, 0)
        block_pos = lax.dynamic_slice_in_dim(positions, start, rows, 0)
        scores = jnp.einsum('qhd,khd->hqk', block_q, keys) * scale
        visible = positions[None, :] <= block_pos[:, None]
        scores = jnp.where(visible[None], scores, -jnp.inf)
        score_tan = (jnp.einsum('qhd,khd->hqk', block_dq, keys) + jnp.einsum('qhd,khd->hqk', block_q, key_dot)) * scale
        probs = jax.nn.softmax(scores, axis=-1)
        weighted = probs * score_tan
        mass = jnp.sum(weighted, axis=-1)
        probs_low = lax.optimization_barrier(probs.astype(jnp.bfloat16)).astype(jnp.float32)
        weighted_low = lax.optimization_barrier(weighted.astype(jnp.bfloat16)).astype(jnp.float32)
        mixed = jnp.einsum('hqk,khd->hqd', probs_low, values)
        tangent = jnp.einsum('hqk,khd->hqd', weighted_low, values) + jnp.einsum('hqk,khd->hqd', probs_low, value_dot)
        tangent = tangent - mass[..., None] * mixed
        mixed = jnp.transpose(mixed, (1, 0, 2)).reshape(rows, HEADS * HEAD_DIM)
        tangent = jnp.transpose(tangent, (1, 0, 2)).reshape(rows, HEADS * HEAD_DIM)
        return mixed.astype(jnp.bfloat16), tangent.astype(jnp.bfloat16)

    starts = (jnp.arange(SEQ // rows) * rows).astype(jnp.int32)
    mixed_all, tangent_all = lax.map(one_block, starts)
    return mixed_all.reshape(SEQ, HEADS * HEAD_DIM), tangent_all.reshape(SEQ, HEADS * HEAD_DIM)
```

```python
import jax
import jax.numpy as jnp
from jax import lax
from jax.experimental import pallas as pl
from jax.experimental.pallas import tpu as pltpu
from jax.sharding import PartitionSpec as P

D = 128
NZ = 16
ROWS = 16
BLOCK = NZ * ROWS
KB = 8
QB = 4
SCALE = D ** -0.5
LOG2E = 1.4426950408889634
CHUNKS = 2
SLOTS = NZ // CHUNKS
CROWS = SLOTS * ROWS
NEG = -1e30
MESH = pl.DeviceIdType.MESH


def offset(i):
    return ((i + 1) // 2) * (2 * (i % 2) - 1)


def kernel(q_ref, k_ref, v_ref, dq_ref, dk_ref, dv_ref, pos_ref,
           out_ref, tan_ref,
           kpack, qpack, prow, kbuf, qbuf, pbuf, kpos, qpos,
           s_buf, p_buf, w_buf,
           part, pstat, opart, ostat, obuf, rbuf,
           zk_send, zk_recv, zq_send, zq_recv, zp_send, zp_recv,
           k_send, k_recv, q_send, q_recv, kp_send, kp_recv, qp_send, qp_recv,
           o_send, o_recv, st_send, st_recv, f_send, f_recv):
    s = lax.axis_index("seq")
    h = lax.axis_index("head")
    c = s % 2
    z = (s // 2) % NZ
    y = (h % 2) * 2 + s // (2 * NZ)
    x = h // 2

    def device(x_, y_, z_, c_):
        return (((y_ % 2) * NZ + z_) * 2 + c_, x_ * 2 + y_ // 2)

    def along_z(by):
        return device(x, y, (z + by + NZ) % NZ, c)

    def along_x(by):
        return device((x + by) % 4, y, z, c)

    def along_y(by):
        return device(x, (y + by) % 4, z, c)

    twin = device(x, y, z, 1 - c)

    barrier = pltpu.get_barrier_semaphore()

    def greet(i, carry):
        pl.semaphore_signal(barrier, inc=1, device_id=along_z(i), device_id_type=MESH)
        return carry

    lax.fori_loop(1, NZ, greet, 0)
    for by in (1, 2, 3):
        pl.semaphore_signal(barrier, inc=1, device_id=along_x(by), device_id_type=MESH)
        pl.semaphore_signal(barrier, inc=1, device_id=along_y(by), device_id_type=MESH)
        pl.semaphore_signal(barrier, inc=1, device_id=device((x + by) % 4, y, z, 1 - c), device_id_type=MESH)
    pl.semaphore_signal(barrier, inc=1, device_id=twin, device_id_type=MESH)

    for head in range(NZ):
        rows = pl.ds(head * ROWS, ROWS)
        cols = pl.ds(head * D, D)
        for at, ref in enumerate((k_ref, dk_ref, v_ref, dv_ref)):
            kpack[rows, at * D:(at + 1) * D] = ref[:, cols]
        for at, ref in enumerate((dq_ref, q_ref)):
            qpack[rows, at * D:(at + 1) * D] = ref[:, cols]
    lane = lax.broadcasted_iota(jnp.int32, (1, D), 1)
    row = jnp.zeros((1, D), jnp.int32)
    for i in range(ROWS):
        row = jnp.where(lane % ROWS == i, pos_ref[i], row)
    prow[...] = row

    pl.semaphore_wait(barrier, NZ - 1 + 10)

    def z_copies(i):
        by = offset(i)
        to = along_z(-by)
        source = pl.ds(pl.multiple_of(((z - by + NZ) % NZ) * ROWS, ROWS), ROWS)
        slot = pl.ds(pl.multiple_of(i * ROWS, ROWS), ROWS)
        return (
            pltpu.make_async_remote_copy(
                kpack.at[source, :], kbuf.at[0, slot, :], zk_send.at[i], zk_recv.at[i],
                device_id=to, device_id_type=MESH),
            pltpu.make_async_remote_copy(
                qpack.at[source, :], qbuf.at[0, slot, :], zq_send.at[i], zq_recv.at[i],
                device_id=to, device_id_type=MESH),
            pltpu.make_async_remote_copy(
                prow, pbuf.at[i], zp_send.at[i], zp_recv.at[i],
                device_id=to, device_id_type=MESH),
        )

    def z_start(i, carry):
        for copy in z_copies(i):
            copy.start()
        return carry

    lax.fori_loop(1, NZ, z_start, 0)
    own = pl.ds(pl.multiple_of(z * ROWS, ROWS), ROWS)
    kbuf[0, 0:ROWS, :] = kpack[own, :]
    qbuf[0, 0:ROWS, :] = qpack[own, :]
    pbuf[0] = prow[...]

    def k_copy(block, rows, to, at, sem):
        return pltpu.make_async_remote_copy(
            kbuf.at[block, rows, :], kbuf.at[at, rows, :], k_send.at[sem], k_recv.at[sem],
            device_id=to, device_id_type=MESH)

    def q_copy(block, rows, to, at, sem):
        return pltpu.make_async_remote_copy(
            qbuf.at[block, rows, :], qbuf.at[at, rows, :], q_send.at[sem], q_recv.at[sem],
            device_id=to, device_id_type=MESH)

    half = CROWS // 2

    def first_copies(g):
        rows = pl.ds(g * CROWS, CROWS)
        return (
            k_copy(0, rows, along_x(1), 6, g * 8 + 6),
            k_copy(0, rows, along_x(3), 2, g * 8 + 2),
            q_copy(0, rows, along_y(1), 3, g * 4 + 3),
            q_copy(0, rows, along_y(3), 1, g * 4 + 1),
            k_copy(0, rows, twin, 1, g * 8 + 1),
        )

    def second_copies(g):
        low = pl.ds(g * CROWS, half)
        high = pl.ds(g * CROWS + half, half)
        rows = pl.ds(g * CROWS, CROWS)
        return (
            k_copy(2, low, along_x(3), 4, g * 8 + 4),
            k_copy(6, high, along_x(1), 4, g * 8 + 0),
            q_copy(1, low, along_y(3), 2, g * 4 + 2),
            q_copy(3, high, along_y(1), 2, g * 4 + 0),
            k_copy(2, rows, twin, 3, g * 8 + 3),
            k_copy(6, rows, twin, 7, g * 8 + 7),
        )

    def third_copies(g):
        return (k_copy(4, pl.ds(g * CROWS, CROWS), twin, 5, g * 8 + 5),)

    def kp_copy(to, at):
        return pltpu.make_async_remote_copy(
            kpos.at[0], kpos.at[at], kp_send.at[at], kp_recv.at[at],
            device_id=to, device_id_type=MESH)

    def qp_copy(to, at):
        return pltpu.make_async_remote_copy(
            kpos.at[0], qpos.at[at], qp_send.at[at], qp_recv.at[at],
            device_id=to, device_id_type=MESH)

    def pos_copies():
        copies = [kp_copy(twin, 1)]
        for by in (1, 2, 3):
            copies.append(kp_copy(along_x(4 - by), 2 * by))
            copies.append(kp_copy(device((x + 4 - by) % 4, y, z, 1 - c), 2 * by + 1))
            copies.append(qp_copy(along_y(4 - by), by))
        return copies

    def stage_one(g):
        def arrive(i, carry):
            for copy in z_copies(i):
                copy.wait_recv()
            return carry

        lax.fori_loop(max(1, g * SLOTS), (g + 1) * SLOTS, arrive, 0)
        for copy in first_copies(g):
            copy.start()

    def stage_two(g):
        for copy in first_copies(g)[:4]:
            copy.wait_recv()
        for copy in second_copies(g):
            copy.start()

    def stage_three(g):
        for copy in second_copies(g)[:4]:
            copy.wait_recv()
        for copy in third_copies(g):
            copy.start()

    for step in range(CHUNKS + 2):
        if step < CHUNKS:
            stage_one(step)
        if step == CHUNKS - 1:
            total = []
            for g in range(2):
                line = jnp.zeros((1, D), jnp.int32)
                for i in range(8):
                    line = jnp.where(lane // ROWS == i, pbuf[g * 8 + i], line)
                total.append(line)
            line = jnp.concatenate(total, axis=1)
            kpos[0] = line
            qpos[0] = line
            for copy in pos_copies():
                copy.start()
        if 0 <= step - 1 < CHUNKS:
            stage_two(step - 1)
        if 0 <= step - 2 < CHUNKS:
            stage_three(step - 2)

    for copy in pos_copies():
        copy.wait_recv()
    for g in range(CHUNKS):
        first_copies(g)[4].wait_recv()
        for copy in second_copies(g)[4:]:
            copy.wait_recv()
        third_copies(g)[0].wait_recv()

    def column(line):
        parts = []
        for at in range(0, BLOCK, D):
            parts.append(jnp.transpose(jnp.broadcast_to(line[:, at:at + D], (D, D))))
        return jnp.concatenate(parts, axis=0)

    def dot_t(a, b):
        return lax.dot_general(a, b, (((1,), (1,)), ((), ())), preferred_element_type=jnp.float32)

    def tile(dy):
        queries = qbuf[dy]
        q_place = column(qpos[dy])[:, 0:1]
        top = jnp.full((BLOCK, D), NEG, jnp.float32)
        for b in range(KB):
            scores = dot_t(queries[:, D:], kbuf[b, :, 0:D])
            scores = jnp.where(kpos[b] <= q_place, scores, NEG)
            s_buf[:, b * BLOCK:(b + 1) * BLOCK] = scores
            top = jnp.maximum(top, jnp.maximum(scores[:, :D], scores[:, D:]))
        top = jnp.max(top, axis=1, keepdims=True)
        total = jnp.zeros((BLOCK, D), jnp.float32)
        mass = jnp.zeros((BLOCK, D), jnp.float32)
        for b in range(KB):
            cols = pl.ds(b * BLOCK, BLOCK)
            expo = jnp.exp2((s_buf[:, cols] - top) * (SCALE * LOG2E))
            weighted = expo * dot_t(queries, kbuf[b, :, 0:2 * D])
            total = total + (expo[:, :D] + expo[:, D:])
            mass = mass + (weighted[:, :D] + weighted[:, D:])
            p_buf[:, cols] = expo.astype(jnp.bfloat16)
            w_buf[:, cols] = weighted.astype(jnp.bfloat16)
        total = jnp.sum(total, axis=1, keepdims=True)
        mass = jnp.sum(mass, axis=1, keepdims=True)
        both = jnp.zeros((BLOCK, 2 * D), jnp.float32)
        third = jnp.zeros((BLOCK, D), jnp.float32)
        for b in range(KB):
            cols = pl.ds(b * BLOCK, BLOCK)
            both = both + jnp.dot(p_buf[:, cols], kbuf[b, :, 2 * D:], preferred_element_type=jnp.float32)
            third = third + jnp.dot(w_buf[:, cols], kbuf[b, :, 2 * D:3 * D], preferred_element_type=jnp.float32)
        inverse = 1.0 / total
        mean = mass * (SCALE * inverse)
        mixed = both[:, :D] * inverse
        tangent = (third * SCALE + both[:, D:]) * inverse - mean * mixed
        lanes = lax.broadcasted_iota(jnp.int32, (BLOCK, D), 1)
        stats = jnp.where(lanes == 0, top * (SCALE * LOG2E), jnp.where(lanes == 1, total, mean))
        stats = jnp.concatenate(
            [jnp.transpose(stats[at:at + D])[0:8] for at in range(0, BLOCK, D)], axis=1)
        return mixed, tangent, stats

    def o_copies(dy):
        to = along_y(dy)
        return (
            pltpu.make_async_remote_copy(
                part.at[dy], opart.at[dy], o_send.at[dy], o_recv.at[dy],
                device_id=to, device_id_type=MESH),
            pltpu.make_async_remote_copy(
                pstat.at[dy], ostat.at[dy], st_send.at[dy], st_recv.at[dy],
                device_id=to, device_id_type=MESH),
        )

    def tile_step(i, carry):
        dy = 4 - i
        mixed, tangent, stats = tile(dy)
        part[dy, :, 0:D] = mixed.astype(jnp.bfloat16)
        part[dy, :, D:] = tangent.astype(jnp.bfloat16)
        pstat[dy] = stats
        for copy in o_copies(dy):
            copy.start()
        return carry

    lax.fori_loop(1, QB, tile_step, 0)
    mixed, tangent, stats = tile(0)

    for dy in (1, 2, 3):
        for copy in o_copies(dy):
            copy.wait_recv()
    tops = [stats[0:1]] + [ostat[dy, 0:1, :] for dy in (1, 2, 3)]
    totals = [stats[1:2]] + [ostat[dy, 1:2, :] for dy in (1, 2, 3)]
    means = [stats[2:3]] + [ostat[dy, 2:3, :] for dy in (1, 2, 3)]
    top = jnp.maximum(jnp.maximum(tops[0], tops[1]), jnp.maximum(tops[2], tops[3]))
    shares = [t * jnp.exp2(m - top) for t, m in zip(totals, tops)]
    inverse = 1.0 / (shares[0] + shares[1] + shares[2] + shares[3])
    shares = [share * inverse for share in shares]
    mean = sum(share * m for share, m in zip(shares, means))
    shifts = [share * (m - mean) for share, m in zip(shares, means)]
    table = jnp.concatenate(shares + shifts + [jnp.zeros((D - 8, BLOCK), jnp.float32)], axis=0)
    table = jnp.concatenate(
        [jnp.transpose(table[:, at:at + D]) for at in range(0, BLOCK, D)], axis=0)
    mixed_all = table[:, 0:1] * mixed
    tangent_all = table[:, 0:1] * tangent + table[:, 4:5] * mixed
    for dy in (1, 2, 3):
        other = opart[dy, :, 0:D].astype(jnp.float32)
        mixed_all = mixed_all + table[:, dy:dy + 1] * other
        tangent_all = tangent_all + (
            table[:, dy:dy + 1] * opart[dy, :, D:].astype(jnp.float32)
            + table[:, 4 + dy:5 + dy] * other)
    obuf[:, 0:D] = mixed_all.astype(jnp.bfloat16)
    obuf[:, D:] = tangent_all.astype(jnp.bfloat16)

    def f_copy(i):
        slot = pl.ds(pl.multiple_of(i * ROWS, ROWS), ROWS)
        return pltpu.make_async_remote_copy(
            obuf.at[slot, :], rbuf.at[i], f_send.at[i], f_recv.at[i],
            device_id=along_z(offset(i)), device_id_type=MESH)

    def f_start(i, carry):
        f_copy(i).start()
        return carry

    lax.fori_loop(1, NZ, f_start, 0)
    rbuf[0] = obuf[0:ROWS, :]

    def drain(i, carry):
        for copy in z_copies(i):
            copy.wait_send()
        return carry

    lax.fori_loop(1, NZ, drain, 0)
    for copy in pos_copies():
        copy.wait_send()
    for g in range(CHUNKS):
        for copy in first_copies(g) + second_copies(g) + third_copies(g):
            copy.wait_send()
    for dy in (1, 2, 3):
        for copy in o_copies(dy):
            copy.wait_send()

    def finish(i, carry):
        f_copy(i).wait_recv()
        cols = pl.ds(pl.multiple_of(((z - offset(i) + NZ) % NZ) * D, D), D)
        out_ref[:, cols] = rbuf[i, :, 0:D]
        tan_ref[:, cols] = rbuf[i, :, D:]
        return carry

    cols = pl.ds(pl.multiple_of(z * D, D), D)
    out_ref[:, cols] = rbuf[0, :, 0:D]
    tan_ref[:, cols] = rbuf[0, :, D:]
    lax.fori_loop(1, NZ, finish, 0)

    def close(i, carry):
        f_copy(i).wait_send()
        return carry

    lax.fori_loop(1, NZ, close, 0)


def local(*args):
    dma = pltpu.SemaphoreType.DMA
    bf16, f32, i32 = jnp.bfloat16, jnp.float32, jnp.int32
    shape = jax.ShapeDtypeStruct((ROWS, NZ * D), bf16)
    return pl.pallas_call(
        kernel,
        out_shape=(shape, shape),
        in_specs=[pl.BlockSpec(memory_space=pltpu.VMEM)] * 6 + [pl.BlockSpec(memory_space=pltpu.SMEM)],
        out_specs=(pl.BlockSpec(memory_space=pltpu.VMEM),) * 2,
        scratch_shapes=[
            pltpu.VMEM((BLOCK, 4 * D), bf16),
            pltpu.VMEM((BLOCK, 2 * D), bf16),
            pltpu.VMEM((1, D), i32),
            pltpu.VMEM((KB, BLOCK, 4 * D), bf16),
            pltpu.VMEM((QB, BLOCK, 2 * D), bf16),
            pltpu.VMEM((NZ, 1, D), i32),
            pltpu.VMEM((KB, 1, BLOCK), i32),
            pltpu.VMEM((QB, 1, BLOCK), i32),
            pltpu.VMEM((BLOCK, KB * BLOCK), f32),
            pltpu.VMEM((BLOCK, KB * BLOCK), bf16),
            pltpu.VMEM((BLOCK, KB * BLOCK), bf16),
            pltpu.VMEM((QB, BLOCK, 2 * D), bf16),
            pltpu.VMEM((QB, 8, BLOCK), f32),
            pltpu.VMEM((QB, BLOCK, 2 * D), bf16),
            pltpu.VMEM((QB, 8, BLOCK), f32),
            pltpu.VMEM((BLOCK, 2 * D), bf16),
            pltpu.VMEM((NZ, ROWS, 2 * D), bf16),
            dma((NZ,)), dma((NZ,)), dma((NZ,)), dma((NZ,)), dma((NZ,)), dma((NZ,)),
            dma((CHUNKS * KB,)), dma((CHUNKS * KB,)), dma((CHUNKS * QB,)), dma((CHUNKS * QB,)),
            dma((KB,)), dma((KB,)), dma((QB,)), dma((QB,)),
            dma((QB,)), dma((QB,)), dma((QB,)), dma((QB,)),
            dma((NZ,)), dma((NZ,)),
        ],
        compiler_params=pltpu.CompilerParams(
            collective_id=0, has_side_effects=True, vmem_limit_bytes=40 * 2 ** 20),
    )(*args)


def solution(mesh):
    rows = P(("seq", "head"), None)
    return jax.shard_map(
        local,
        mesh=mesh,
        in_specs=(rows,) * 6 + (P(("seq", "head")),),
        out_specs=(rows, rows),
        check_vma=False,
    )
```

```python
import jax
import jax.numpy as jnp
from jax import lax
from jax.experimental import pallas as pl
from jax.experimental.pallas import tpu as pltpu
from jax.sharding import PartitionSpec as P

D = 128
NZ = 16
ROWS = 16
BLOCK = NZ * ROWS
HALF = BLOCK // 2
KB = 8
QB = 4
SCALE = D ** -0.5
LOG2E = 1.4426950408889634
NEG = -1e30
MESH = pl.DeviceIdType.MESH
DISTANCES = (2, 1, 3, 0)
OWN = NZ - 1


def offset(slot):
    i = NZ - 1 - slot
    return ((i + 1) // 2) * (2 * (i % 2) - 1)


def loop(start, stop, body):
    def step(i, carry):
        body(i)
        return carry

    lax.fori_loop(start, stop, step, 0)


def dot_t(a, b):
    return lax.dot_general(a, b, (((1,), (1,)), ((), ())), preferred_element_type=jnp.float32)


def kernel(q_hbm, k_hbm, v_hbm, dq_hbm, dk_hbm, dv_hbm, pos_hbm,
           out_ref, tan_ref,
           q_ref, k_ref, v_ref, dq_ref, dk_ref, dv_ref, pos_ref, in_sem,
           kpack, vpack, qpack, prow, kbuf, vbuf, qbuf, pbuf, kpos, qpos,
           s_buf, p_buf, w_buf, part, pstat, opart, ostat, obuf, rbuf,
           zk_send, zk_recv, zv_send, zv_recv, zq_send, zq_recv, zp_send, zp_recv,
           k_send, k_recv, v_send, v_recv, q_send, q_recv,
           kp_send, kp_recv, qp_send, qp_recv,
           o_send, o_recv, st_send, st_recv, f_send, f_recv):
    s = lax.axis_index("seq")
    h = lax.axis_index("head")
    c = s % 2
    z = (s // 2) % NZ
    y = (h % 2) * 2 + s // (2 * NZ)
    x = h // 2

    def device(x_, y_, z_, c_):
        return (((y_ % 2) * NZ + z_) * 2 + c_, x_ * 2 + y_ // 2)

    def along_z(by):
        return device(x, y, (z + by + NZ) % NZ, c)

    def along_x(by):
        return device((x + by) % 4, y, z, c)

    def across_x(by):
        return device((x + by) % 4, y, z, 1 - c)

    def along_y(by):
        return device(x, (y + by) % 4, z, c)

    twin = device(x, y, z, 1 - c)

    def send(source, target, send_sem, recv_sem, to):
        return pltpu.make_async_remote_copy(
            source, target, send_sem, recv_sem, device_id=to, device_id_type=MESH)

    fetches = [
        pltpu.make_async_copy(source, held, in_sem.at[i])
        for i, (source, held) in enumerate((
            (k_hbm, k_ref), (dk_hbm, dk_ref), (pos_hbm, pos_ref), (v_hbm, v_ref), (dv_hbm, dv_ref),
            (dq_hbm, dq_ref), (q_hbm, q_ref)))
    ]
    for fetch in fetches:
        fetch.start()

    barrier = pltpu.get_barrier_semaphore()

    def greet(to):
        pl.semaphore_signal(barrier, inc=1, device_id=to, device_id_type=MESH)

    loop(1, NZ, lambda i: greet(along_z(i)))
    for by in (1, 2, 3):
        greet(along_x(by))
        greet(across_x(by))
        greet(along_y(by))
    greet(twin)

    own = pl.ds(pl.multiple_of(z * ROWS, ROWS), ROWS)

    def pack(left, right, packed, place):
        for head in range(NZ):
            rows = pl.ds(head * ROWS, ROWS)
            cols = pl.ds(head * D, D)
            packed[rows, 0:D] = left[:, cols]
            packed[rows, D:] = right[:, cols]
        place[...] = packed[own, :]

    for fetch in fetches[:3]:
        fetch.wait()
    pack(k_ref, dk_ref, kpack, kbuf.at[0, OWN * ROWS:, :])
    lane = lax.broadcasted_iota(jnp.int32, (1, D), 1)
    row = jnp.zeros((1, D), jnp.int32)
    for i in range(ROWS):
        row = jnp.where(lane % ROWS == i, pos_ref[i], row)
    prow[...] = row
    pbuf[OWN] = row

    pl.semaphore_wait(barrier, NZ - 1 + 10)

    def z_copy(packed, buf, send_sem, recv_sem, i):
        by = offset(i)
        source = pl.ds(pl.multiple_of(((z - by + NZ) % NZ) * ROWS, ROWS), ROWS)
        slot = pl.ds(pl.multiple_of(i * ROWS, ROWS), ROWS)
        if buf is qbuf:
            slot = pl.ds(pl.multiple_of(3 * HALF + (i % 8) * ROWS, ROWS), ROWS)
            target = buf.at[i // 8, slot, :]
        else:
            target = buf.at[0, slot, :]
        return send(packed.at[source, :], target, send_sem.at[i], recv_sem.at[i], along_z(-by))

    def zk(i):
        return z_copy(kpack, kbuf, zk_send, zk_recv, i)

    def zv(i):
        return z_copy(vpack, vbuf, zv_send, zv_recv, i)

    def zq(i):
        return z_copy(qpack, qbuf, zq_send, zq_recv, i)

    def zp(i):
        return send(prow, pbuf.at[i], zp_send.at[i], zp_recv.at[i], along_z(-offset(i)))

    def gather(buf, send_sem, recv_sem):
        def copy(block, rows, to, at, sem):
            return send(buf.at[block, rows, :], buf.at[at, rows, :], send_sem.at[sem], recv_sem.at[sem], to)

        every = pl.ds(0, BLOCK)
        first = lambda: [
            copy(0, every, along_x(2), 4, 4),
            copy(0, every, along_x(1), 6, 6),
            copy(0, every, along_x(3), 2, 2),
            copy(0, every, twin, 1, 1),
        ]
        second = lambda: [copy(block, every, twin, block + 1, block + 1) for block in (2, 6, 4)]
        return first, second

    k_first, k_second = gather(kbuf, k_send, k_recv)
    v_first, v_second = gather(vbuf, v_send, v_recv)

    def group(dy):
        return pl.ds(DISTANCES.index(dy) * HALF, HALF)

    def q_copy(half, dy):
        sem = half * 4 + dy
        return send(qbuf.at[half, group(0), :], qbuf.at[half, group(dy), :],
                    q_send.at[sem], q_recv.at[sem], along_y(4 - dy))

    def q_copies(half):
        return [q_copy(half, dy) for dy in (2, 1, 3)]

    def kp_copy(to, at):
        return send(kpos.at[0], kpos.at[at], kp_send.at[at], kp_recv.at[at], to)

    def qp_copy(to, at):
        return send(kpos.at[0], qpos.at[at], qp_send.at[at], qp_recv.at[at], to)

    def pos_copies():
        copies = [kp_copy(twin, 1)]
        for by in (1, 2, 3):
            copies.append(kp_copy(along_x(4 - by), 2 * by))
            copies.append(kp_copy(across_x(4 - by), 2 * by + 1))
            copies.append(qp_copy(along_y(4 - by), by))
        return copies

    def start_all(copies):
        for copy in copies:
            copy.start()

    def wait_recv_all(copies):
        for copy in copies:
            copy.wait_recv()

    def first_z(i):
        zk(i).start()
        zp(i).start()

    loop(0, OWN, first_z)
    for fetch in fetches[3:5]:
        fetch.wait()
    pack(v_ref, dv_ref, vpack, vbuf.at[0, OWN * ROWS:, :])

    def values_z(i):
        zk(i).wait_send()
        zv(i).start()

    def queries_z(i):
        zv(i).wait_send()
        zq(i).start()

    loop(0, OWN, values_z)
    for fetch in fetches[5:]:
        fetch.wait()
    pack(dq_ref, q_ref, qpack, qbuf.at[1, 4 * HALF - ROWS:, :])
    loop(0, OWN, lambda i: zk(i).wait_recv())
    start_all(k_first())
    loop(0, OWN, lambda i: zp(i).wait_recv())
    total = []
    for g in range(2):
        line = jnp.zeros((1, D), jnp.int32)
        for i in range(8):
            line = jnp.where(lane // ROWS == i, pbuf[g * 8 + i], line)
        total.append(line)
    line = jnp.concatenate(total, axis=1)
    kpos[0] = line
    qpos[0] = line
    start_all(pos_copies())
    loop(0, OWN, queries_z)
    wait_recv_all(k_first()[:3])
    start_all(k_second())
    loop(0, OWN, lambda i: zv(i).wait_recv())
    start_all(v_first())
    loop(0, NZ // 2, lambda i: zq(i).wait_recv())
    start_all(q_copies(0))
    loop(NZ // 2, OWN, lambda i: zq(i).wait_recv())
    start_all(q_copies(1))
    wait_recv_all(v_first()[:3])
    start_all(v_second())
    wait_recv_all(pos_copies())
    wait_recv_all(k_first()[3:] + k_second())
    wait_recv_all(v_first()[3:] + v_second())

    def tile(half, pair):
        rows = pl.ds(pl.multiple_of(pair * BLOCK, BLOCK), BLOCK)
        queries = qbuf[half, rows, :]
        dys = (DISTANCES[0] + pair * (DISTANCES[2] - DISTANCES[0]), DISTANCES[1] + pair * (DISTANCES[3] - DISTANCES[1]))
        places = []
        for dy in dys:
            line = qpos[dy, :, pl.ds(pl.multiple_of(half * HALF, HALF), HALF)]
            places.append(jnp.transpose(jnp.broadcast_to(line, (HALF, HALF))))
        places = jnp.concatenate(places, axis=0)[:, 0:1]
        top = jnp.full((BLOCK, D), NEG, jnp.float32)
        for b in range(KB):
            scores = dot_t(queries[:, D:], kbuf[b, :, 0:D])
            scores = jnp.where(kpos[b] <= places, scores, NEG)
            s_buf[:, b * BLOCK:(b + 1) * BLOCK] = scores
            top = jnp.maximum(top, jnp.maximum(scores[:, :D], scores[:, D:]))
        top = jnp.max(top, axis=1, keepdims=True)
        total = jnp.zeros((BLOCK, D), jnp.float32)
        mass = jnp.zeros((BLOCK, D), jnp.float32)
        for b in range(KB):
            cols = pl.ds(b * BLOCK, BLOCK)
            expo = jnp.exp2((s_buf[:, cols] - top) * (SCALE * LOG2E))
            weighted = expo * dot_t(queries, kbuf[b])
            total = total + (expo[:, :D] + expo[:, D:])
            mass = mass + (weighted[:, :D] + weighted[:, D:])
            p_buf[:, cols] = expo.astype(jnp.bfloat16)
            w_buf[:, cols] = weighted.astype(jnp.bfloat16)
        total = jnp.sum(total, axis=1, keepdims=True)
        mass = jnp.sum(mass, axis=1, keepdims=True)
        both = jnp.zeros((BLOCK, 2 * D), jnp.float32)
        third = jnp.zeros((BLOCK, D), jnp.float32)
        for b in range(KB):
            cols = pl.ds(b * BLOCK, BLOCK)
            both = both + jnp.dot(p_buf[:, cols], vbuf[b], preferred_element_type=jnp.float32)
            third = third + jnp.dot(w_buf[:, cols], vbuf[b, :, 0:D], preferred_element_type=jnp.float32)
        inverse = 1.0 / total
        mean = mass * (SCALE * inverse)
        mixed = both[:, :D] * inverse
        tangent = (third * SCALE + both[:, D:]) * inverse - mean * mixed
        lanes = lax.broadcasted_iota(jnp.int32, (BLOCK, D), 1)
        stats = jnp.where(lanes == 0, top * (SCALE * LOG2E), jnp.where(lanes == 1, total, mean))
        part[half, rows, 0:D] = mixed.astype(jnp.bfloat16)
        part[half, rows, D:] = tangent.astype(jnp.bfloat16)
        for at, dy in enumerate(dys):
            pstat[half * 4 + dy] = jnp.transpose(stats[at * HALF:(at + 1) * HALF])[0:8]

    def o_copy(half, dy):
        sem = half * 4 + dy
        return send(part.at[half, group(dy), :], opart.at[half, group(dy), :],
                    o_send.at[sem], o_recv.at[sem], along_y(dy))

    def st_copy(half, dy):
        sem = half * 4 + dy
        return send(pstat.at[sem], ostat.at[sem], st_send.at[sem], st_recv.at[sem], along_y(dy))

    def f_copy(i):
        slot = pl.ds(pl.multiple_of(i * ROWS, ROWS), ROWS)
        return send(obuf.at[slot, :], rbuf.at[i], f_send.at[i], f_recv.at[i], along_z(offset(i)))

    def merge(half):
        for dy in (1, 2, 3):
            o_copy(half, dy).wait_recv()
            st_copy(half, dy).wait_recv()
        rows = pl.ds(half * HALF, HALF)
        lines = [pstat[half * 4]] + [ostat[half * 4 + dy] for dy in (1, 2, 3)]
        tops = [line[0:1] for line in lines]
        top = jnp.maximum(jnp.maximum(tops[0], tops[1]), jnp.maximum(tops[2], tops[3]))
        shares = [line[1:2] * jnp.exp2(line[0:1] - top) for line in lines]
        inverse = 1.0 / (shares[0] + shares[1] + shares[2] + shares[3])
        shares = [share * inverse for share in shares]
        mean = sum(share * line[2:3] for share, line in zip(shares, lines))
        shifts = [share * (line[2:3] - mean) for share, line in zip(shares, lines)]
        table = jnp.concatenate(shares + shifts + [jnp.zeros((D - 8, HALF), jnp.float32)], axis=0)
        table = jnp.transpose(table)
        mixed = jnp.zeros((HALF, D), jnp.float32)
        tangent = jnp.zeros((HALF, D), jnp.float32)
        for dy in range(QB):
            held = part if dy == 0 else opart
            one = held[half, group(dy), 0:D].astype(jnp.float32)
            two = held[half, group(dy), D:].astype(jnp.float32)
            mixed = mixed + table[:, dy:dy + 1] * one
            tangent = tangent + (table[:, dy:dy + 1] * two + table[:, 4 + dy:5 + dy] * one)
        obuf[rows, 0:D] = mixed.astype(jnp.bfloat16)
        obuf[rows, D:] = tangent.astype(jnp.bfloat16)
        loop(half * NZ // 2, min(OWN, (half + 1) * NZ // 2), lambda i: f_copy(i).start())

    def o_start(half, dy):
        o_copy(half, dy).start()
        st_copy(half, dy).start()

    def tile_step(i):
        half = i // 2
        pair = i % 2

        @pl.when(pair == 0)
        def _():
            q_copy(half, 2).wait_recv()
            q_copy(half, 1).wait_recv()

        @pl.when(pair == 1)
        def _():
            q_copy(half, 3).wait_recv()

        tile(half, pair)

        @pl.when(pair == 0)
        def _():
            o_start(half, 2)
            o_start(half, 1)

        @pl.when(pair == 1)
        def _():
            o_start(half, 3)

    loop(0, 4, tile_step)
    merge(0)
    merge(1)

    def drain(i):
        for copy in (zp(i), zq(i)):
            copy.wait_send()

    loop(0, OWN, drain)
    sent = pos_copies() + k_first() + k_second() + v_first() + v_second()
    for half in range(2):
        sent += q_copies(half)
        for dy in (1, 2, 3):
            sent += [o_copy(half, dy), st_copy(half, dy)]
    for copy in sent:
        copy.wait_send()

    def place(head, held):
        cols = pl.ds(pl.multiple_of(head * D, D), D)
        out_ref[:, cols] = held[:, 0:D]
        tan_ref[:, cols] = held[:, D:]

    place(z, obuf[OWN * ROWS:, :])

    def finish(i):
        f_copy(i).wait_recv()
        place((z - offset(i) + NZ) % NZ, rbuf[i])

    loop(0, OWN, finish)
    loop(0, OWN, lambda i: f_copy(i).wait_send())


def local(*args):
    dma = pltpu.SemaphoreType.DMA
    bf16, f32, i32 = jnp.bfloat16, jnp.float32, jnp.int32
    shape = jax.ShapeDtypeStruct((ROWS, NZ * D), bf16)
    return pl.pallas_call(
        kernel,
        out_shape=(shape, shape),
        in_specs=[pl.BlockSpec(memory_space=pl.ANY)] * 7,
        out_specs=(pl.BlockSpec(memory_space=pltpu.VMEM),) * 2,
        scratch_shapes=[pltpu.VMEM((ROWS, NZ * D), bf16)] * 6 + [
            pltpu.SMEM((ROWS,), i32),
            dma((7,)),
            pltpu.VMEM((BLOCK, 2 * D), bf16),
            pltpu.VMEM((BLOCK, 2 * D), bf16),
            pltpu.VMEM((BLOCK, 2 * D), bf16),
            pltpu.VMEM((1, D), i32),
            pltpu.VMEM((KB, BLOCK, 2 * D), bf16),
            pltpu.VMEM((KB, BLOCK, 2 * D), bf16),
            pltpu.VMEM((2, QB * HALF, 2 * D), bf16),
            pltpu.VMEM((NZ, 1, D), i32),
            pltpu.VMEM((KB, 1, BLOCK), i32),
            pltpu.VMEM((QB, 1, BLOCK), i32),
            pltpu.VMEM((BLOCK, KB * BLOCK), f32),
            pltpu.VMEM((BLOCK, KB * BLOCK), bf16),
            pltpu.VMEM((BLOCK, KB * BLOCK), bf16),
            pltpu.VMEM((2, QB * HALF, 2 * D), bf16),
            pltpu.VMEM((2 * QB, 8, HALF), f32),
            pltpu.VMEM((2, QB * HALF, 2 * D), bf16),
            pltpu.VMEM((2 * QB, 8, HALF), f32),
            pltpu.VMEM((BLOCK, 2 * D), bf16),
            pltpu.VMEM((NZ, ROWS, 2 * D), bf16),
        ] + [dma((NZ,))] * 8 + [dma((KB,))] * 4 + [dma((2 * QB,))] * 2
        + [dma((KB,))] * 2 + [dma((QB,))] * 2 + [dma((2 * QB,))] * 4 + [dma((NZ,))] * 2,
        compiler_params=pltpu.CompilerParams(
            collective_id=0, has_side_effects=True, vmem_limit_bytes=40 * 2 ** 20),
    )(*args)


def solution(mesh):
    rows = P(("seq", "head"), None)
    return jax.shard_map(
        local,
        mesh=mesh,
        in_specs=(rows,) * 6 + (P(("seq", "head")),),
        out_specs=(rows, rows),
        check_vma=False,
    )
```

```python
import jax
import jax.numpy as jnp
from jax import lax
from jax.experimental import pallas as pl
from jax.experimental.pallas import tpu as pltpu
from jax.sharding import PartitionSpec as P

D = 128
NZ = 16
ROWS = 16
BLOCK = NZ * ROWS
HALF = BLOCK // 2
PART = BLOCK // 4
SLOTS = NZ // 4
KB = 8
QB = 4
SCALE = D ** -0.5
LOG2E = 1.4426950408889634
NEG = -1e30
MESH = pl.DeviceIdType.MESH
DISTANCES = (2, 1, 3, 0)
OWN = NZ - 1


def offset(slot):
    i = NZ - 1 - slot
    return ((i + 1) // 2) * (2 * (i % 2) - 1)


def loop(start, stop, body):
    def step(i, carry):
        body(i)
        return carry

    lax.fori_loop(start, stop, step, 0)


def dot_t(a, b):
    return lax.dot_general(a, b, (((1,), (1,)), ((), ())), preferred_element_type=jnp.float32)


def kernel(q_hbm, k_hbm, v_hbm, dq_hbm, dk_hbm, dv_hbm, pos_hbm,
           out_ref, tan_ref,
           q_ref, k_ref, v_ref, dq_ref, dk_ref, dv_ref, pos_ref, in_sem,
           kpack, vpack, qpack, prow, kbuf, vbuf, qbuf, pbuf, kpos, qpos, qcol,
           s_buf, p_buf, w_buf, part, pstat, opart, ostat, obuf, rbuf,
           zk_send, zk_recv, zv_send, zv_recv, zq_send, zq_recv, zp_send, zp_recv,
           k_send, k_recv, v_send, v_recv, q_send, q_recv,
           kp_send, kp_recv, qp_send, qp_recv,
           o_send, o_recv, st_send, st_recv, f_send, f_recv):
    s = lax.axis_index("seq")
    h = lax.axis_index("head")
    c = s % 2
    z = (s // 2) % NZ
    y = (h % 2) * 2 + s // (2 * NZ)
    x = h // 2

    def device(x_, y_, z_, c_):
        return (((y_ % 2) * NZ + z_) * 2 + c_, x_ * 2 + y_ // 2)

    def along_z(by):
        return device(x, y, (z + by + NZ) % NZ, c)

    def along_x(by):
        return device((x + by) % 4, y, z, c)

    def across_x(by):
        return device((x + by) % 4, y, z, 1 - c)

    def along_y(by):
        return device(x, (y + by) % 4, z, c)

    twin = device(x, y, z, 1 - c)

    def send(source, target, send_sem, recv_sem, to):
        return pltpu.make_async_remote_copy(
            source, target, send_sem, recv_sem, device_id=to, device_id_type=MESH)

    fetches = [
        pltpu.make_async_copy(source, held, in_sem.at[i])
        for i, (source, held) in enumerate((
            (k_hbm, k_ref), (dk_hbm, dk_ref), (pos_hbm, pos_ref), (v_hbm, v_ref), (dv_hbm, dv_ref),
            (dq_hbm, dq_ref), (q_hbm, q_ref)))
    ]
    for fetch in fetches:
        fetch.start()

    barrier = pltpu.get_barrier_semaphore()

    def greet(to):
        pl.semaphore_signal(barrier, inc=1, device_id=to, device_id_type=MESH)

    loop(1, NZ, lambda i: greet(along_z(i)))
    for by in (1, 2, 3):
        greet(along_x(by))
        greet(across_x(by))
        greet(along_y(by))
    greet(twin)

    own = pl.ds(pl.multiple_of(z * ROWS, ROWS), ROWS)

    def pack(left, right, packed, place):
        for head in range(NZ):
            rows = pl.ds(head * ROWS, ROWS)
            cols = pl.ds(head * D, D)
            packed[rows, 0:D] = left[:, cols]
            packed[rows, D:] = right[:, cols]
        place[...] = packed[own, :]

    for fetch in fetches[:3]:
        fetch.wait()
    pack(k_ref, dk_ref, kpack, kbuf.at[0, OWN * ROWS:, :])
    lane = lax.broadcasted_iota(jnp.int32, (1, D), 1)
    row = jnp.zeros((1, D), jnp.int32)
    for i in range(ROWS):
        row = jnp.where(lane % ROWS == i, pos_ref[i], row)
    prow[...] = row
    pbuf[OWN] = row

    pl.semaphore_wait(barrier, NZ - 1 + 10)

    def arrived(ref, sem):
        pltpu.make_async_copy(ref, ref, sem).wait()

    def z_copy(packed, buf, send_sem, recv_sem, i):
        by = offset(i)
        source = pl.ds(pl.multiple_of(((z - by + NZ) % NZ) * ROWS, ROWS), ROWS)
        slot = pl.ds(pl.multiple_of(i * ROWS, ROWS), ROWS)
        if buf is qbuf:
            slot = pl.ds(pl.multiple_of(3 * PART + (i % SLOTS) * ROWS, ROWS), ROWS)
            target = buf.at[i // SLOTS, slot, :]
        else:
            target = buf.at[0, slot, :]
        shared = i // SLOTS if buf is qbuf else i // (NZ // 2)
        return send(packed.at[source, :], target, send_sem.at[i], recv_sem.at[shared], along_z(-by))

    def zk(i):
        return z_copy(kpack, kbuf, zk_send, zk_recv, i)

    def zv(i):
        return z_copy(vpack, vbuf, zv_send, zv_recv, i)

    def zq(i):
        return z_copy(qpack, qbuf, zq_send, zq_recv, i)

    def zp(i):
        return send(prow, pbuf.at[i], zp_send, zp_recv, along_z(-offset(i)))

    def gather(buf, send_sem, recv_sem):
        def copy(block, rows, to, at, sem):
            return send(buf.at[block, rows, :], buf.at[at, rows, :], send_sem, recv_sem.at[sem], to)

        def first(half):
            rows = pl.ds(half * HALF, HALF)
            return [
                copy(0, rows, along_x(2), 4, half),
                copy(0, rows, along_x(1), 6, half),
                copy(0, rows, along_x(3), 2, half),
                copy(0, rows, twin, 1, 2),
            ]

        def first_arrived(half):
            arrived(buf.at[0:3, half * HALF:(half + 1) * HALF, :], recv_sem.at[half])

        def second(half):
            rows = pl.ds(half * HALF, HALF)
            return [copy(block, rows, twin, block + 1, 2) for block in (2, 6, 4)]

        def second_arrived():
            arrived(buf.at[0:4], recv_sem.at[2])

        def left():
            arrived(buf.at[0:7], send_sem)

        return first, first_arrived, second, second_arrived, left

    k_first, k_first_arrived, k_second, k_second_arrived, k_left = gather(kbuf, k_send, k_recv)
    v_first, v_first_arrived, v_second, v_second_arrived, v_left = gather(vbuf, v_send, v_recv)

    def group(dy):
        return pl.ds(DISTANCES.index(dy) * PART, PART)

    def q_copy(quarter, dy):
        return send(qbuf.at[quarter, group(0), :], qbuf.at[quarter, group(dy), :],
                    q_send, q_recv.at[quarter], along_y(4 - dy))

    def q_copies(quarter):
        return [q_copy(quarter, dy) for dy in (2, 1, 3)]

    def kp_copy(to, at):
        return send(kpos.at[0], kpos.at[at], kp_send, kp_recv, to)

    def qp_copy(to, at):
        return send(kpos.at[0], qpos.at[at], qp_send, qp_recv, to)

    def pos_copies():
        copies = [kp_copy(twin, 1)]
        for by in (1, 2, 3):
            copies.append(kp_copy(along_x(4 - by), 2 * by))
            copies.append(kp_copy(across_x(4 - by), 2 * by + 1))
            copies.append(qp_copy(along_y(4 - by), by))
        return copies

    def start_all(copies):
        for copy in copies:
            copy.start()

    def first_z(i):
        zk(i).start()
        zp(i).start()

    loop(0, OWN, first_z)
    for fetch in fetches[3:5]:
        fetch.wait()
    pack(v_ref, dv_ref, vpack, vbuf.at[0, OWN * ROWS:, :])

    def values_z(i):
        zk(i).wait_send()
        zv(i).start()

    def queries_z(i):
        zv(i).wait_send()
        zq(i).start()

    loop(0, OWN, values_z)
    for fetch in fetches[5:]:
        fetch.wait()
    pack(dq_ref, q_ref, qpack, qbuf.at[3, BLOCK - ROWS:, :])
    arrived(kbuf.at[0, 0:HALF, :], zk_recv.at[0])
    start_all(k_first(0))
    arrived(pbuf.at[0:OWN], zp_recv)
    total = []
    for g in range(2):
        line = jnp.zeros((1, D), jnp.int32)
        for i in range(8):
            line = jnp.where(lane // ROWS == i, pbuf[g * 8 + i], line)
        total.append(line)
    line = jnp.concatenate(total, axis=1)
    kpos[0] = line
    qpos[0] = line
    start_all(pos_copies())
    arrived(kbuf.at[0, HALF:OWN * ROWS, :], zk_recv.at[1])
    start_all(k_first(1))
    loop(0, NZ // 2, queries_z)
    k_first_arrived(0)
    start_all(k_second(0))
    loop(NZ // 2, OWN, queries_z)
    arrived(vbuf.at[0, 0:HALF, :], zv_recv.at[0])
    start_all(v_first(0))
    arrived(vbuf.at[0, HALF:OWN * ROWS, :], zv_recv.at[1])
    start_all(v_first(1))
    k_first_arrived(1)
    start_all(k_second(1))
    for quarter in range(4):
        rows = PART if quarter < 3 else PART - ROWS
        arrived(qbuf.at[quarter, 3 * PART:3 * PART + rows, :], zq_recv.at[quarter])
        start_all(q_copies(quarter))
        if quarter == 0:
            v_first_arrived(0)
            start_all(v_second(0))
    arrived(kpos.at[0:7], kp_recv)
    arrived(qpos.at[0:3], qp_recv)
    for dy in range(QB):
        for half in range(2):
            line = qpos[dy, :, half * HALF:(half + 1) * HALF]
            line = jnp.transpose(jnp.broadcast_to(line, (HALF, HALF)))
            qcol[2 * half, group(dy), :] = line[0:PART]
            qcol[2 * half + 1, group(dy), :] = line[PART:]
    v_first_arrived(1)
    start_all(v_second(1))
    k_second_arrived()
    v_second_arrived()

    def tile(quarter):
        queries = qbuf[quarter]
        places = qcol[quarter]
        top = jnp.full((BLOCK, D), NEG, jnp.float32)
        for b in range(KB):
            scores = dot_t(queries[:, D:], kbuf[b, :, 0:D])
            for at in range(0, BLOCK, D):
                side = jnp.where(kpos[b, :, at:at + D] <= places, scores[:, at:at + D], NEG)
                s_buf[:, b * BLOCK + at:b * BLOCK + at + D] = side
                top = jnp.maximum(top, side)
        top = jnp.max(top, axis=1, keepdims=True)
        total = jnp.zeros((BLOCK, D), jnp.float32)
        mass = jnp.zeros((BLOCK, D), jnp.float32)
        for b in range(KB):
            cols = pl.ds(b * BLOCK, BLOCK)
            expo = jnp.exp2((s_buf[:, cols] - top) * (SCALE * LOG2E))
            weighted = expo * dot_t(queries, kbuf[b])
            total = total + (expo[:, :D] + expo[:, D:])
            mass = mass + (weighted[:, :D] + weighted[:, D:])
            p_buf[:, cols] = expo.astype(jnp.bfloat16)
            w_buf[:, cols] = weighted.astype(jnp.bfloat16)
        total = jnp.sum(total, axis=1, keepdims=True)
        mass = jnp.sum(mass, axis=1, keepdims=True)
        both = jnp.zeros((BLOCK, 2 * D), jnp.float32)
        third = jnp.zeros((BLOCK, D), jnp.float32)
        for b in range(KB):
            cols = pl.ds(b * BLOCK, BLOCK)
            both = both + jnp.dot(p_buf[:, cols], vbuf[b], preferred_element_type=jnp.float32)
            third = third + jnp.dot(w_buf[:, cols], vbuf[b, :, 0:D], preferred_element_type=jnp.float32)
        inverse = 1.0 / total
        mean = mass * (SCALE * inverse)
        mixed = both[:, :D] * inverse
        tangent = (third * SCALE + both[:, D:]) * inverse - mean * mixed
        lanes = lax.broadcasted_iota(jnp.int32, (BLOCK, D), 1)
        stats = jnp.where(lanes == 0, top * (SCALE * LOG2E), jnp.where(lanes == 1, total, mean))
        part[quarter, :, 0:D] = mixed.astype(jnp.bfloat16)
        part[quarter, :, D:] = tangent.astype(jnp.bfloat16)
        for at in range(2):
            pstat[quarter * 2 + at] = jnp.transpose(stats[at * HALF:(at + 1) * HALF])[0:8]

    def o_copy(quarter, dy):
        return send(part.at[quarter, group(dy), :], opart.at[quarter, group(dy), :],
                    o_send, o_recv.at[quarter], along_y(dy))

    def st_copy(quarter, dy):
        return send(pstat.at[quarter * 2 + DISTANCES.index(dy) // 2], ostat.at[quarter * 4 + dy],
                    st_send, st_recv.at[quarter], along_y(dy))

    def f_copy(i):
        slot = pl.ds(pl.multiple_of(i * ROWS, ROWS), ROWS)
        return send(obuf.at[slot, :], rbuf.at[i], f_send, f_recv, along_z(offset(i)))

    def merge(quarter):
        arrived(part.at[quarter, 0:3 * PART, :], o_recv.at[quarter])
        arrived(pstat.at[0:3], st_recv.at[quarter])
        lines = []
        for dy in range(QB):
            line = pstat[quarter * 2 + 1] if dy == 0 else ostat[quarter * 4 + dy]
            lines.append(pltpu.roll(line, PART, 1) if DISTANCES.index(dy) % 2 else line)
        tops = [line[0:1] for line in lines]
        top = jnp.maximum(jnp.maximum(tops[0], tops[1]), jnp.maximum(tops[2], tops[3]))
        shares = [line[1:2] * jnp.exp2(line[0:1] - top) for line in lines]
        inverse = 1.0 / (shares[0] + shares[1] + shares[2] + shares[3])
        shares = [share * inverse for share in shares]
        mean = sum(share * line[2:3] for share, line in zip(shares, lines))
        shifts = [share * (line[2:3] - mean) for share, line in zip(shares, lines)]
        table = jnp.concatenate(shares + shifts + [jnp.zeros((D - 8, HALF), jnp.float32)], axis=0)
        table = jnp.transpose(table)
        table = table[0:PART]
        mixed = jnp.zeros((PART, D), jnp.float32)
        tangent = jnp.zeros((PART, D), jnp.float32)
        for dy in range(QB):
            held = part if dy == 0 else opart
            one = held[quarter, group(dy), 0:D].astype(jnp.float32)
            two = held[quarter, group(dy), D:].astype(jnp.float32)
            mixed = mixed + table[:, dy:dy + 1] * one
            tangent = tangent + (table[:, dy:dy + 1] * two + table[:, 4 + dy:5 + dy] * one)
        rows = pl.ds(pl.multiple_of(quarter * PART, PART), PART)
        obuf[rows, 0:D] = mixed.astype(jnp.bfloat16)
        obuf[rows, D:] = tangent.astype(jnp.bfloat16)

        def f_start(i):
            @pl.when(i < OWN)
            def _():
                f_copy(i).start()

        loop(quarter * SLOTS, (quarter + 1) * SLOTS, f_start)

    def step(i):
        @pl.when(i < 4)
        def _():
            arrived(qbuf.at[i, 0:3 * PART, :], q_recv.at[i])
            tile(i)
            for dy in (2, 1, 3):
                o_copy(i, dy).start()
                st_copy(i, dy).start()

        @pl.when(i >= 2)
        def _():
            merge(i - 2)

    loop(0, 6, step)

    loop(0, OWN, lambda i: zq(i).wait_send())
    arrived(pbuf.at[0:OWN], zp_send)
    arrived(kpos.at[0:7], kp_send)
    arrived(qpos.at[0:3], qp_send)
    k_left()
    v_left()
    arrived(qbuf.at[:, 0:3 * PART, :], q_send)
    arrived(part.at[:, 0:3 * PART, :], o_send)
    arrived(ostat.at[0:12], st_send)

    def place(head, held):
        cols = pl.ds(pl.multiple_of(head * D, D), D)
        out_ref[:, cols] = held[:, 0:D]
        tan_ref[:, cols] = held[:, D:]

    place(z, obuf[OWN * ROWS:, :])

    def finish(i):
        place((z - offset(i) + NZ) % NZ, rbuf[i])

    arrived(rbuf.at[0:OWN], f_recv)
    loop(0, OWN, finish)
    arrived(rbuf.at[0:OWN], f_send)


def local(*args):
    dma = pltpu.SemaphoreType.DMA
    bf16, f32, i32 = jnp.bfloat16, jnp.float32, jnp.int32
    return pl.pallas_call(
        kernel,
        out_shape=(pltpu.VMEM((ROWS, NZ * D), bf16),) * 2,
        in_specs=[pl.BlockSpec(memory_space=pl.ANY)] * 7,
        out_specs=(pl.BlockSpec(memory_space=pltpu.VMEM),) * 2,
        scratch_shapes=[pltpu.VMEM((ROWS, NZ * D), bf16)] * 6 + [
            pltpu.SMEM((ROWS,), i32),
            dma((7,)),
            pltpu.VMEM((BLOCK, 2 * D), bf16),
            pltpu.VMEM((BLOCK, 2 * D), bf16),
            pltpu.VMEM((BLOCK, 2 * D), bf16),
            pltpu.VMEM((1, D), i32),
            pltpu.VMEM((KB, BLOCK, 2 * D), bf16),
            pltpu.VMEM((KB, BLOCK, 2 * D), bf16),
            pltpu.VMEM((4, BLOCK, 2 * D), bf16),
            pltpu.VMEM((NZ, 1, D), i32),
            pltpu.VMEM((KB, 1, BLOCK), i32),
            pltpu.VMEM((QB, 1, BLOCK), i32),
            pltpu.VMEM((4, BLOCK, D), i32),
            pltpu.VMEM((BLOCK, KB * BLOCK), f32),
            pltpu.VMEM((BLOCK, KB * BLOCK), bf16),
            pltpu.VMEM((BLOCK, KB * BLOCK), bf16),
            pltpu.VMEM((4, BLOCK, 2 * D), bf16),
            pltpu.VMEM((8, 8, HALF), f32),
            pltpu.VMEM((4, BLOCK, 2 * D), bf16),
            pltpu.VMEM((4 * QB, 8, HALF), f32),
            pltpu.VMEM((BLOCK, 2 * D), bf16),
            pltpu.VMEM((NZ, ROWS, 2 * D), bf16),
        ] + [
            dma((NZ,)), dma((2,)), dma((NZ,)), dma((2,)), dma((NZ,)), dma((4,)), dma, dma,
            dma, dma((3,)), dma, dma((3,)), dma, dma((4,)), dma, dma, dma, dma,
            dma, dma((4,)), dma, dma((4,)), dma, dma,
        ],
        compiler_params=pltpu.CompilerParams(
            collective_id=0, has_side_effects=True, vmem_limit_bytes=62 * 2 ** 20),
    )(*args)


def solution(mesh):
    rows = P(("seq", "head"), None)
    return jax.shard_map(
        local,
        mesh=mesh,
        in_specs=(rows,) * 6 + (P(("seq", "head")),),
        out_specs=(rows, rows),
        check_vma=False,
    )
```

```python
import jax
import jax.numpy as jnp
from jax import lax
from jax.experimental import pallas as pl
from jax.experimental.pallas import tpu as pltpu
from jax.sharding import PartitionSpec as P

D = 128
NZ = 16
ROWS = 16
BLOCK = NZ * ROWS
HALF = BLOCK // 2
PART = BLOCK // 4
SLOTS = NZ // 4
KB = 8
QB = 4
SCALE = D ** -0.5
LOG2E = 1.4426950408889634
NEG = -1e30
MESH = pl.DeviceIdType.MESH
DISTANCES = (2, 1, 3, 0)
OWN = NZ - 1


def offset(slot):
    i = NZ - 1 - slot
    return ((i + 1) // 2) * (2 * (i % 2) - 1)


def loop(start, stop, body):
    def step(i, carry):
        body(i)
        return carry

    lax.fori_loop(start, stop, step, 0)


def dot_t(a, b):
    return lax.dot_general(a, b, (((1,), (1,)), ((), ())), preferred_element_type=jnp.float32)


def kernel(q_hbm, k_hbm, v_hbm, dq_hbm, dk_hbm, dv_hbm, pos_hbm,
           out_ref, tan_ref,
           q_ref, k_ref, v_ref, dq_ref, dk_ref, dv_ref, pos_ref, in_sem,
           kpack, vpack, qpack, prow, kbuf, vbuf, qbuf, pbuf, kpos, qpos, qcol,
           s_buf, p_buf, w_buf, part, pstat, opart, ostat, obuf, rbuf,
           zk_send, zk_recv, zv_send, zv_recv, zq_send, zq_recv, zp_send, zp_recv,
           k_send, k_recv, v_send, v_recv, q_send, q_recv,
           kp_send, kp_recv, qp_send, qp_recv,
           o_send, o_recv, st_send, st_recv, f_send, f_recv):
    s = lax.axis_index("seq")
    h = lax.axis_index("head")
    c = s % 2
    z = (s // 2) % NZ
    y = (h % 2) * 2 + s // (2 * NZ)
    x = h // 2

    def device(x_, y_, z_, c_):
        return (((y_ % 2) * NZ + z_) * 2 + c_, x_ * 2 + y_ // 2)

    def along_z(by):
        return device(x, y, (z + by + NZ) % NZ, c)

    def along_x(by):
        return device((x + by) % 4, y, z, c)

    def across_x(by):
        return device((x + by) % 4, y, z, 1 - c)

    def along_y(by):
        return device(x, (y + by) % 4, z, c)

    twin = device(x, y, z, 1 - c)

    def send(source, target, send_sem, recv_sem, to):
        return pltpu.make_async_remote_copy(
            source, target, send_sem, recv_sem, device_id=to, device_id_type=MESH)

    fetches = [
        pltpu.make_async_copy(source, held, in_sem.at[i])
        for i, (source, held) in enumerate((
            (k_hbm, k_ref), (dk_hbm, dk_ref), (pos_hbm, pos_ref), (v_hbm, v_ref), (dv_hbm, dv_ref),
            (dq_hbm, dq_ref), (q_hbm, q_ref)))
    ]
    for fetch in fetches:
        fetch.start()

    barrier = pltpu.get_barrier_semaphore()

    def greet(to):
        pl.semaphore_signal(barrier, inc=1, device_id=to, device_id_type=MESH)

    loop(0, OWN, lambda i: greet(along_z(offset(i))))
    for by in (1, 2, 3):
        greet(along_x(by))
        greet(across_x(by))
        greet(along_y(by))
    greet(twin)

    own = pl.ds(pl.multiple_of(z * ROWS, ROWS), ROWS)

    def pack(left, right, packed, place):
        for head in range(NZ):
            rows = pl.ds(head * ROWS, ROWS)
            cols = pl.ds(head * D, D)
            packed[rows, 0:D] = left[:, cols]
            packed[rows, D:] = right[:, cols]
        place[...] = packed[own, :]

    for fetch in fetches[:3]:
        fetch.wait()
    pack(k_ref, dk_ref, kpack, kbuf.at[0, OWN * ROWS:, :])
    lane = lax.broadcasted_iota(jnp.int32, (1, D), 1)
    row = jnp.zeros((1, D), jnp.int32)
    for i in range(ROWS):
        row = jnp.where(lane % ROWS == i, pos_ref[i], row)
    prow[...] = row
    pbuf[OWN] = row

    pl.semaphore_wait(barrier, NZ - 1 + 10)

    def arrived(ref, sem):
        pltpu.make_async_copy(ref, ref, sem).wait()

    def z_copy(packed, buf, send_sem, recv_sem, i):
        by = offset(i)
        source = pl.ds(pl.multiple_of(((z - by + NZ) % NZ) * ROWS, ROWS), ROWS)
        slot = pl.ds(pl.multiple_of(i * ROWS, ROWS), ROWS)
        if buf is qbuf:
            slot = pl.ds(pl.multiple_of(3 * PART + (i % SLOTS) * ROWS, ROWS), ROWS)
            target = buf.at[i // SLOTS, slot, :]
        else:
            target = buf.at[0, slot, :]
        shared = i // SLOTS if buf is qbuf else i // (NZ // 2)
        return send(packed.at[source, :], target, send_sem.at[i], recv_sem.at[shared], along_z(-by))

    def zk(i):
        return z_copy(kpack, kbuf, zk_send, zk_recv, i)

    def zv(i):
        return z_copy(vpack, vbuf, zv_send, zv_recv, i)

    def zq(i):
        return z_copy(qpack, qbuf, zq_send, zq_recv, i)

    def zp(i):
        return send(prow, pbuf.at[i], zp_send, zp_recv, along_z(-offset(i)))

    def gather(buf, send_sem, recv_sem):
        def copy(block, rows, to, at, sem):
            return send(buf.at[block, rows, :], buf.at[at, rows, :], send_sem, recv_sem.at[sem], to)

        def first(half):
            rows = pl.ds(half * HALF, HALF)
            return [
                copy(0, rows, along_x(2), 4, half),
                copy(0, rows, along_x(1), 6, half),
                copy(0, rows, along_x(3), 2, half),
                copy(0, rows, twin, 1, 2),
            ]

        def first_arrived(half):
            arrived(buf.at[0:3, half * HALF:(half + 1) * HALF, :], recv_sem.at[half])

        def second(half):
            rows = pl.ds(half * HALF, HALF)
            return [copy(block, rows, twin, block + 1, 2) for block in (2, 6, 4)]

        def second_arrived():
            arrived(buf.at[0:4], recv_sem.at[2])

        def left():
            arrived(buf.at[0:7], send_sem)

        return first, first_arrived, second, second_arrived, left

    k_first, k_first_arrived, k_second, k_second_arrived, k_left = gather(kbuf, k_send, k_recv)
    v_first, v_first_arrived, v_second, v_second_arrived, v_left = gather(vbuf, v_send, v_recv)

    def group(dy):
        return pl.ds(DISTANCES.index(dy) * PART, PART)

    def q_copy(quarter, dy):
        return send(qbuf.at[quarter, group(0), :], qbuf.at[quarter, group(dy), :],
                    q_send, q_recv.at[quarter], along_y(4 - dy))

    def q_copies(quarter):
        return [q_copy(quarter, dy) for dy in (2, 1, 3)]

    def kp_copy(to, at):
        return send(kpos.at[0], kpos.at[at], kp_send, kp_recv, to)

    def qp_copy(to, at):
        return send(kpos.at[0], qpos.at[at], qp_send, qp_recv, to)

    def pos_copies():
        copies = [kp_copy(twin, 1)]
        for by in (1, 2, 3):
            copies.append(kp_copy(along_x(4 - by), 2 * by))
            copies.append(kp_copy(across_x(4 - by), 2 * by + 1))
            copies.append(qp_copy(along_y(4 - by), by))
        return copies

    def start_all(copies):
        for copy in copies:
            copy.start()

    def first_z(i):
        zk(i).start()
        zp(i).start()

    loop(0, OWN, first_z)
    for fetch in fetches[3:5]:
        fetch.wait()
    pack(v_ref, dv_ref, vpack, vbuf.at[0, OWN * ROWS:, :])

    def values_z(i):
        zk(i).wait_send()
        zv(i).start()

    def queries_z(i):
        zv(i).wait_send()
        zq(i).start()

    loop(0, OWN, values_z)
    for fetch in fetches[5:]:
        fetch.wait()
    pack(dq_ref, q_ref, qpack, qbuf.at[3, BLOCK - ROWS:, :])
    arrived(kbuf.at[0, 0:HALF, :], zk_recv.at[0])
    start_all(k_first(0))
    arrived(pbuf.at[0:OWN], zp_recv)
    total = []
    for g in range(2):
        line = jnp.zeros((1, D), jnp.int32)
        for i in range(8):
            line = jnp.where(lane // ROWS == i, pbuf[g * 8 + i], line)
        total.append(line)
    line = jnp.concatenate(total, axis=1)
    kpos[0] = line
    qpos[0] = line
    start_all(pos_copies())
    arrived(kbuf.at[0, HALF:OWN * ROWS, :], zk_recv.at[1])
    start_all(k_first(1))
    loop(0, NZ // 2, queries_z)
    k_first_arrived(0)
    start_all(k_second(0))
    loop(NZ // 2, OWN, queries_z)
    arrived(vbuf.at[0, 0:HALF, :], zv_recv.at[0])
    start_all(v_first(0))
    arrived(vbuf.at[0, HALF:OWN * ROWS, :], zv_recv.at[1])
    start_all(v_first(1))
    k_first_arrived(1)
    start_all(k_second(1))
    arrived(kpos.at[0:7], kp_recv)
    arrived(qpos.at[0:3], qp_recv)
    for dy in range(QB):
        for half in range(2):
            line = qpos[dy, :, half * HALF:(half + 1) * HALF]
            line = jnp.transpose(jnp.broadcast_to(line, (HALF, HALF)))
            qcol[2 * half, group(dy), :] = line[0:PART]
            qcol[2 * half + 1, group(dy), :] = line[PART:]
    for quarter in range(4):
        rows = PART if quarter < 3 else PART - ROWS
        arrived(qbuf.at[quarter, 3 * PART:3 * PART + rows, :], zq_recv.at[quarter])
        start_all(q_copies(quarter))
        if quarter == 0:
            v_first_arrived(0)
            start_all(v_second(0))
    v_first_arrived(1)
    start_all(v_second(1))
    k_second_arrived()

    def score(quarter, side):
        queries = qbuf[quarter]
        places = qcol[quarter]
        top = jnp.full((BLOCK, D), NEG, jnp.float32)
        for b in range(KB):
            scores = dot_t(queries[:, D:], kbuf[b, :, 0:D])
            for at in range(0, BLOCK, D):
                seen = jnp.where(kpos[b, :, at:at + D] <= places, scores[:, at:at + D], NEG)
                s_buf[:, b * BLOCK + at:b * BLOCK + at + D] = seen
                top = jnp.maximum(top, seen)
        top = jnp.max(top, axis=1, keepdims=True)
        total = jnp.zeros((BLOCK, D), jnp.float32)
        for b in range(KB):
            cols = pl.ds(b * BLOCK, BLOCK)
            expo = jnp.exp2((s_buf[:, cols] - top) * (SCALE * LOG2E))
            weighted = expo * dot_t(queries, kbuf[b])
            total = total + (expo[:, :D] + expo[:, D:])
            p_buf[side, :, cols] = expo.astype(jnp.bfloat16)
            w_buf[side, :, cols] = weighted.astype(jnp.bfloat16)
        return top, jnp.sum(total, axis=1, keepdims=True)

    def mix(quarter, side, top, total):
        both = jnp.zeros((BLOCK, 2 * D), jnp.float32)
        third = jnp.zeros((BLOCK, 2 * D), jnp.float32)
        ones = jnp.ones((BLOCK, D), jnp.bfloat16)
        for b in range(KB):
            cols = pl.ds(b * BLOCK, BLOCK)
            both = both + jnp.dot(p_buf[side, :, cols], vbuf[b], preferred_element_type=jnp.float32)
            third = third + jnp.dot(
                w_buf[side, :, cols], jnp.concatenate([vbuf[b, :, 0:D], ones], axis=1),
                preferred_element_type=jnp.float32)
        inverse = 1.0 / total
        mean = third[:, D:] * (SCALE * inverse)
        mixed = both[:, :D] * inverse
        tangent = (third[:, :D] * SCALE + both[:, D:]) * inverse - mean * mixed
        lanes = lax.broadcasted_iota(jnp.int32, (BLOCK, D), 1)
        stats = jnp.where(lanes == 0, top * (SCALE * LOG2E), jnp.where(lanes == 1, total, mean))
        part[quarter, :, 0:D] = mixed.astype(jnp.bfloat16)
        part[quarter, :, D:] = tangent.astype(jnp.bfloat16)
        for at in range(2):
            pstat[quarter * 2 + at] = jnp.transpose(stats[at * HALF:(at + 1) * HALF])[0:8]

    def o_copy(quarter, dy):
        return send(part.at[quarter, group(dy), :], opart.at[quarter, group(dy), :],
                    o_send, o_recv.at[quarter], along_y(dy))

    def st_copy(quarter, dy):
        return send(pstat.at[quarter * 2 + DISTANCES.index(dy) // 2], ostat.at[quarter * 4 + dy],
                    st_send, st_recv.at[quarter], along_y(dy))

    def f_copy(i):
        slot = pl.ds(pl.multiple_of(i * ROWS, ROWS), ROWS)
        return send(obuf.at[slot, :], rbuf.at[i], f_send, f_recv, along_z(offset(i)))

    def merge(quarter):
        arrived(part.at[quarter, 0:3 * PART, :], o_recv.at[quarter])
        arrived(pstat.at[0:3], st_recv.at[quarter])
        lines = []
        for dy in range(QB):
            line = pstat[quarter * 2 + 1] if dy == 0 else ostat[quarter * 4 + dy]
            lines.append(pltpu.roll(line, PART, 1) if DISTANCES.index(dy) % 2 else line)
        tops = [line[0:1] for line in lines]
        top = jnp.maximum(jnp.maximum(tops[0], tops[1]), jnp.maximum(tops[2], tops[3]))
        shares = [line[1:2] * jnp.exp2(line[0:1] - top) for line in lines]
        inverse = 1.0 / (shares[0] + shares[1] + shares[2] + shares[3])
        shares = [share * inverse for share in shares]
        mean = sum(share * line[2:3] for share, line in zip(shares, lines))
        shifts = [share * (line[2:3] - mean) for share, line in zip(shares, lines)]
        table = jnp.concatenate(shares + shifts + [jnp.zeros((D - 8, HALF), jnp.float32)], axis=0)
        table = jnp.transpose(table)
        table = table[0:PART]
        mixed = jnp.zeros((PART, D), jnp.float32)
        tangent = jnp.zeros((PART, D), jnp.float32)
        for dy in range(QB):
            held = part if dy == 0 else opart
            one = held[quarter, group(dy), 0:D].astype(jnp.float32)
            two = held[quarter, group(dy), D:].astype(jnp.float32)
            mixed = mixed + table[:, dy:dy + 1] * one
            tangent = tangent + (table[:, dy:dy + 1] * two + table[:, 4 + dy:5 + dy] * one)
        rows = pl.ds(pl.multiple_of(quarter * PART, PART), PART)
        obuf[rows, 0:D] = mixed.astype(jnp.bfloat16)
        obuf[rows, D:] = tangent.astype(jnp.bfloat16)

        def f_start(i):
            @pl.when(i < OWN)
            def _():
                f_copy(i).start()

        loop(quarter * SLOTS, (quarter + 1) * SLOTS, f_start)

    def q_arrived(quarter):
        arrived(qbuf.at[quarter, 0:3 * PART, :], q_recv.at[quarter])

    def o_start(quarter):
        for dy in (2, 1, 3):
            o_copy(quarter, dy).start()
            st_copy(quarter, dy).start()

    q_arrived(0)
    held = score(0, 0)
    v_second_arrived()

    def step(i, held):
        q_arrived(i + 1)
        mix(i, i % 2, *held)
        o_start(i)
        held = score(i + 1, (i + 1) % 2)
        return held

    held = lax.fori_loop(0, 3, step, held)
    mix(3, 1, *held)
    o_start(3)
    loop(0, 4, merge)

    loop(0, OWN, lambda i: zq(i).wait_send())
    arrived(pbuf.at[0:OWN], zp_send)
    arrived(kpos.at[0:7], kp_send)
    arrived(qpos.at[0:3], qp_send)
    k_left()
    v_left()
    arrived(qbuf.at[:, 0:3 * PART, :], q_send)
    arrived(part.at[:, 0:3 * PART, :], o_send)
    arrived(ostat.at[0:12], st_send)

    def place(head, held):
        cols = pl.ds(pl.multiple_of(head * D, D), D)
        out_ref[:, cols] = held[:, 0:D]
        tan_ref[:, cols] = held[:, D:]

    place(z, obuf[OWN * ROWS:, :])

    def finish(i):
        place((z - offset(i) + NZ) % NZ, rbuf[i])

    arrived(rbuf.at[0:OWN], f_recv)
    loop(0, OWN, finish)
    arrived(rbuf.at[0:OWN], f_send)


def local(*args):
    dma = pltpu.SemaphoreType.DMA
    bf16, f32, i32 = jnp.bfloat16, jnp.float32, jnp.int32
    return pl.pallas_call(
        kernel,
        out_shape=(pltpu.VMEM((ROWS, NZ * D), bf16),) * 2,
        in_specs=[pl.BlockSpec(memory_space=pl.ANY)] * 7,
        out_specs=(pl.BlockSpec(memory_space=pltpu.VMEM),) * 2,
        scratch_shapes=[pltpu.VMEM((ROWS, NZ * D), bf16)] * 6 + [
            pltpu.SMEM((ROWS,), i32),
            dma((7,)),
            pltpu.VMEM((BLOCK, 2 * D), bf16),
            pltpu.VMEM((BLOCK, 2 * D), bf16),
            pltpu.VMEM((BLOCK, 2 * D), bf16),
            pltpu.VMEM((1, D), i32),
            pltpu.VMEM((KB, BLOCK, 2 * D), bf16),
            pltpu.VMEM((KB, BLOCK, 2 * D), bf16),
            pltpu.VMEM((4, BLOCK, 2 * D), bf16),
            pltpu.VMEM((NZ, 1, D), i32),
            pltpu.VMEM((KB, 1, BLOCK), i32),
            pltpu.VMEM((QB, 1, BLOCK), i32),
            pltpu.VMEM((4, BLOCK, D), i32),
            pltpu.VMEM((BLOCK, KB * BLOCK), f32),
            pltpu.VMEM((2, BLOCK, KB * BLOCK), bf16),
            pltpu.VMEM((2, BLOCK, KB * BLOCK), bf16),
            pltpu.VMEM((4, BLOCK, 2 * D), bf16),
            pltpu.VMEM((8, 8, HALF), f32),
            pltpu.VMEM((4, BLOCK, 2 * D), bf16),
            pltpu.VMEM((4 * QB, 8, HALF), f32),
            pltpu.VMEM((BLOCK, 2 * D), bf16),
            pltpu.VMEM((NZ, ROWS, 2 * D), bf16),
        ] + [
            dma((NZ,)), dma((2,)), dma((NZ,)), dma((2,)), dma((NZ,)), dma((4,)), dma, dma,
            dma, dma((3,)), dma, dma((3,)), dma, dma((4,)), dma, dma, dma, dma,
            dma, dma((4,)), dma, dma((4,)), dma, dma,
        ],
        compiler_params=pltpu.CompilerParams(
            collective_id=0, has_side_effects=True, vmem_limit_bytes=62 * 2 ** 20),
    )(*args)


def solution(mesh):
    rows = P(("seq", "head"), None)
    return jax.shard_map(
        local,
        mesh=mesh,
        in_specs=(rows,) * 6 + (P(("seq", "head")),),
        out_specs=(rows, rows),
        check_vma=False,
    )
```

```python
import jax
import jax.numpy as jnp
from jax import lax
from jax.experimental import pallas as pl
from jax.experimental.pallas import tpu as pltpu
from jax.sharding import PartitionSpec as P

D = 128
NZ = 16
ROWS = 16
BLOCK = NZ * ROWS
HALF = BLOCK // 2
PART = BLOCK // 4
OTHERS = 3 * PART
SLOTS = NZ // 4
KB = 8
QB = 4
SCALE = D ** -0.5
LOG2E = 1.4426950408889634
NEG = -1e30
MESH = pl.DeviceIdType.MESH
DISTANCES = (2, 1, 3)
OWN = NZ - 1


def offset(slot):
    i = NZ - 1 - slot
    return ((i + 1) // 2) * (2 * (i % 2) - 1)


def loop(start, stop, body):
    def step(i, carry):
        body(i)
        return carry

    lax.fori_loop(start, stop, step, 0)


def dot_t(a, b):
    return lax.dot_general(a, b, (((1,), (1,)), ((), ())), preferred_element_type=jnp.float32)


def kernel(q_hbm, k_hbm, v_hbm, dq_hbm, dk_hbm, dv_hbm, pos_hbm,
           out_ref, tan_ref,
           q_ref, k_ref, v_ref, dq_ref, dk_ref, dv_ref, pos_ref, in_sem,
           kpack, vpack, qpack, prow, kbuf, vbuf, qown, qoth, pbuf, kpos, qpos, owncol, othcol,
           s_buf, p_buf, w_buf, mine, mstat, part, pstat, opart, ostat, obuf, rbuf,
           zk_send, zk_recv, zv_send, zv_recv, zq_send, zq_recv, zp_send, zp_recv,
           k_send, k_recv, v_send, v_recv, q_send, q_recv,
           kp_send, kp_recv, qp_send, qp_recv,
           o_send, o_recv, st_send, st_recv, f_send, f_recv):
    s = lax.axis_index("seq")
    h = lax.axis_index("head")
    c = s % 2
    z = (s // 2) % NZ
    y = (h % 2) * 2 + s // (2 * NZ)
    x = h // 2

    def device(x_, y_, z_, c_):
        return (((y_ % 2) * NZ + z_) * 2 + c_, x_ * 2 + y_ // 2)

    def along_z(by):
        return device(x, y, (z + by + NZ) % NZ, c)

    def along_x(by):
        return device((x + by) % 4, y, z, c)

    def across_x(by):
        return device((x + by) % 4, y, z, 1 - c)

    def along_y(by):
        return device(x, (y + by) % 4, z, c)

    twin = device(x, y, z, 1 - c)

    def send(source, target, send_sem, recv_sem, to):
        return pltpu.make_async_remote_copy(
            source, target, send_sem, recv_sem, device_id=to, device_id_type=MESH)

    fetches = [
        pltpu.make_async_copy(source, held, in_sem.at[i])
        for i, (source, held) in enumerate((
            (k_hbm, k_ref), (dk_hbm, dk_ref), (pos_hbm, pos_ref), (v_hbm, v_ref), (dv_hbm, dv_ref),
            (dq_hbm, dq_ref), (q_hbm, q_ref)))
    ]
    for fetch in fetches:
        fetch.start()

    barrier = pltpu.get_barrier_semaphore()

    def greet(to):
        pl.semaphore_signal(barrier, inc=1, device_id=to, device_id_type=MESH)

    loop(0, OWN, lambda i: greet(along_z(offset(i))))
    for by in (1, 2, 3):
        greet(along_x(by))
        greet(across_x(by))
        greet(along_y(by))
    greet(twin)

    own = pl.ds(pl.multiple_of(z * ROWS, ROWS), ROWS)

    def pack(left, right, packed, place):
        for head in range(NZ):
            rows = pl.ds(head * ROWS, ROWS)
            cols = pl.ds(head * D, D)
            packed[rows, 0:D] = left[:, cols]
            packed[rows, D:] = right[:, cols]
        place[...] = packed[own, :]

    for fetch in fetches[:3]:
        fetch.wait()
    pack(k_ref, dk_ref, kpack, kbuf.at[0, OWN * ROWS:, :])
    lane = lax.broadcasted_iota(jnp.int32, (1, D), 1)
    row = jnp.zeros((1, D), jnp.int32)
    for i in range(ROWS):
        row = jnp.where(lane % ROWS == i, pos_ref[i], row)
    prow[...] = row
    pbuf[OWN] = row

    pl.semaphore_wait(barrier, NZ - 1 + 10)

    def arrived(ref, sem):
        pltpu.make_async_copy(ref, ref, sem).wait()

    def z_copy(packed, buf, send_sem, recv_sem, i):
        by = offset(i)
        source = pl.ds(pl.multiple_of(((z - by + NZ) % NZ) * ROWS, ROWS), ROWS)
        slot = pl.ds(pl.multiple_of(i * ROWS, ROWS), ROWS)
        target = buf.at[slot, :] if buf is qown else buf.at[0, slot, :]
        shared = i // SLOTS if buf is qown else i // (NZ // 2)
        return send(packed.at[source, :], target, send_sem.at[i], recv_sem.at[shared], along_z(-by))

    def zk(i):
        return z_copy(kpack, kbuf, zk_send, zk_recv, i)

    def zv(i):
        return z_copy(vpack, vbuf, zv_send, zv_recv, i)

    def zq(i):
        return z_copy(qpack, qown, zq_send, zq_recv, i)

    def zp(i):
        return send(prow, pbuf.at[i], zp_send, zp_recv, along_z(-offset(i)))

    def gather(buf, send_sem, recv_sem):
        def copy(block, rows, to, at, sem):
            return send(buf.at[block, rows, :], buf.at[at, rows, :], send_sem, recv_sem.at[sem], to)

        def first(half):
            rows = pl.ds(half * HALF, HALF)
            return [
                copy(0, rows, along_x(2), 4, half),
                copy(0, rows, along_x(1), 6, half),
                copy(0, rows, along_x(3), 2, half),
                copy(0, rows, twin, 1, 2),
            ]

        def first_arrived(half):
            arrived(buf.at[0:3, half * HALF:(half + 1) * HALF, :], recv_sem.at[half])

        def second(half):
            rows = pl.ds(half * HALF, HALF)
            return [copy(block, rows, twin, block + 1, 2) for block in (2, 6, 4)]

        def second_arrived():
            arrived(buf.at[0:4], recv_sem.at[2])

        def left():
            arrived(buf.at[0:7], send_sem)

        return first, first_arrived, second, second_arrived, left

    k_first, k_first_arrived, k_second, k_second_arrived, k_left = gather(kbuf, k_send, k_recv)
    v_first, v_first_arrived, v_second, v_second_arrived, v_left = gather(vbuf, v_send, v_recv)

    def group(dy):
        return pl.ds(DISTANCES.index(dy) * PART, PART)

    def q_copy(quarter, dy):
        return send(qown.at[quarter * PART:(quarter + 1) * PART, :], qoth.at[quarter, group(dy), :],
                    q_send, q_recv.at[quarter], along_y(4 - dy))

    def q_copies(quarter):
        return [q_copy(quarter, dy) for dy in (2, 1, 3)]

    def kp_copy(to, at):
        return send(kpos.at[0], kpos.at[at], kp_send, kp_recv, to)

    def qp_copy(to, at):
        return send(kpos.at[0], qpos.at[at], qp_send, qp_recv, to)

    def pos_copies():
        copies = [kp_copy(twin, 1)]
        for by in (1, 2, 3):
            copies.append(kp_copy(along_x(4 - by), 2 * by))
            copies.append(kp_copy(across_x(4 - by), 2 * by + 1))
            copies.append(qp_copy(along_y(4 - by), by))
        return copies

    def start_all(copies):
        for copy in copies:
            copy.start()

    def first_z(i):
        zk(i).start()
        zp(i).start()

    loop(0, OWN, first_z)
    for fetch in fetches[3:5]:
        fetch.wait()
    pack(v_ref, dv_ref, vpack, vbuf.at[0, OWN * ROWS:, :])

    loop(0, OWN, lambda i: zv(i).start())
    for fetch in fetches[5:]:
        fetch.wait()
    pack(dq_ref, q_ref, qpack, qown.at[OWN * ROWS:, :])
    loop(0, OWN, lambda i: zq(i).start())
    arrived(kbuf.at[0, 0:HALF, :], zk_recv.at[0])
    start_all(k_first(0))
    arrived(pbuf.at[0:OWN], zp_recv)
    total = []
    for g in range(2):
        line = jnp.zeros((1, D), jnp.int32)
        for i in range(8):
            line = jnp.where(lane // ROWS == i, pbuf[g * 8 + i], line)
        total.append(line)
    line = jnp.concatenate(total, axis=1)
    kpos[0] = line
    qpos[0] = line
    start_all(pos_copies())
    arrived(kbuf.at[0, HALF:OWN * ROWS, :], zk_recv.at[1])
    start_all(k_first(1))
    k_first_arrived(0)
    start_all(k_second(0))
    arrived(vbuf.at[0, 0:HALF, :], zv_recv.at[0])
    start_all(v_first(0))
    arrived(vbuf.at[0, HALF:OWN * ROWS, :], zv_recv.at[1])
    start_all(v_first(1))
    k_first_arrived(1)
    start_all(k_second(1))
    arrived(kpos.at[0:7], kp_recv)
    arrived(qpos.at[0:3], qp_recv)
    for dy in range(QB):
        for half in range(2):
            line = qpos[dy, :, half * HALF:(half + 1) * HALF]
            line = jnp.transpose(jnp.broadcast_to(line, (HALF, HALF)))
            if dy == 0:
                owncol[half * HALF:(half + 1) * HALF, :] = line
            else:
                othcol[2 * half, group(dy), :] = line[0:PART]
                othcol[2 * half + 1, group(dy), :] = line[PART:]
    for quarter in range(4):
        rows = PART if quarter < 3 else PART - ROWS
        arrived(qown.at[quarter * PART:quarter * PART + rows, :], zq_recv.at[quarter])
        start_all(q_copies(quarter))
        if quarter == 0:
            v_first_arrived(0)
            start_all(v_second(0))
    v_first_arrived(1)
    start_all(v_second(1))
    k_second_arrived()

    def score(queries, places, side):
        rows = queries.shape[0]
        top = jnp.full((rows, D), NEG, jnp.float32)
        for b in range(KB):
            scores = dot_t(queries[:, D:], kbuf[b, :, 0:D])
            for at in range(0, BLOCK, D):
                seen = jnp.where(kpos[b, :, at:at + D] <= places, scores[:, at:at + D], NEG)
                s_buf[0:rows, b * BLOCK + at:b * BLOCK + at + D] = seen
                top = jnp.maximum(top, seen)
        top = jnp.max(top, axis=1, keepdims=True)
        total = jnp.zeros((rows, D), jnp.float32)
        for b in range(KB):
            cols = pl.ds(b * BLOCK, BLOCK)
            expo = jnp.exp2((s_buf[0:rows, cols] - top) * (SCALE * LOG2E))
            weighted = expo * dot_t(queries, kbuf[b])
            total = total + (expo[:, :D] + expo[:, D:])
            p_buf[side, 0:rows, cols] = expo.astype(jnp.bfloat16)
            w_buf[side, 0:rows, cols] = weighted.astype(jnp.bfloat16)
        return top, jnp.sum(total, axis=1, keepdims=True)

    def mix(held, stats_held, side, top, total):
        rows = held.shape[0]
        both = jnp.zeros((rows, 2 * D), jnp.float32)
        third = jnp.zeros((rows, 2 * D), jnp.float32)
        ones = jnp.ones((BLOCK, D), jnp.bfloat16)
        for b in range(KB):
            cols = pl.ds(b * BLOCK, BLOCK)
            both = both + jnp.dot(p_buf[side, 0:rows, cols], vbuf[b], preferred_element_type=jnp.float32)
            third = third + jnp.dot(
                w_buf[side, 0:rows, cols], jnp.concatenate([vbuf[b, :, 0:D], ones], axis=1),
                preferred_element_type=jnp.float32)
        inverse = 1.0 / total
        mean = third[:, D:] * (SCALE * inverse)
        mixed = both[:, :D] * inverse
        tangent = (third[:, :D] * SCALE + both[:, D:]) * inverse - mean * mixed
        lanes = lax.broadcasted_iota(jnp.int32, (rows, D), 1)
        stats = jnp.where(lanes == 0, top * (SCALE * LOG2E), jnp.where(lanes == 1, total, mean))
        held[:, 0:D] = mixed.astype(jnp.bfloat16)
        held[:, D:] = tangent.astype(jnp.bfloat16)
        stats_held[0] = jnp.transpose(stats[0:D])[0:8]
        rest = stats[D:]
        if rows < BLOCK:
            rest = jnp.concatenate([rest, rest], axis=0)
        stats_held[1] = jnp.transpose(rest)[0:8]

    def o_copy(quarter, dy):
        return send(part.at[quarter, group(dy), :], opart.at[quarter, group(dy), :],
                    o_send, o_recv.at[quarter], along_y(dy))

    def st_copy(quarter, dy):
        return send(pstat.at[quarter * 2 + DISTANCES.index(dy) // 2], ostat.at[quarter * 4 + dy],
                    st_send, st_recv.at[quarter], along_y(dy))

    def f_copy(i):
        slot = pl.ds(pl.multiple_of(i * ROWS, ROWS), ROWS)
        return send(obuf.at[slot, :], rbuf.at[i], f_send, f_recv, along_z(offset(i)))

    def merge(quarter):
        arrived(part.at[quarter], o_recv.at[quarter])
        arrived(pstat.at[0:3], st_recv.at[quarter])
        line = mstat[quarter // 2]
        lines = [jnp.where(quarter % 2 == 1, pltpu.roll(line, PART, 1), line)]
        for dy in (1, 2, 3):
            line = ostat[quarter * 4 + dy]
            lines.append(pltpu.roll(line, PART, 1) if DISTANCES.index(dy) % 2 else line)
        tops = [line[0:1] for line in lines]
        top = jnp.maximum(jnp.maximum(tops[0], tops[1]), jnp.maximum(tops[2], tops[3]))
        shares = [line[1:2] * jnp.exp2(line[0:1] - top) for line in lines]
        inverse = 1.0 / (shares[0] + shares[1] + shares[2] + shares[3])
        shares = [share * inverse for share in shares]
        mean = sum(share * line[2:3] for share, line in zip(shares, lines))
        shifts = [share * (line[2:3] - mean) for share, line in zip(shares, lines)]
        table = jnp.concatenate(shares + shifts + [jnp.zeros((D - 8, HALF), jnp.float32)], axis=0)
        table = jnp.transpose(table)
        table = table[0:PART]
        rows = pl.ds(pl.multiple_of(quarter * PART, PART), PART)
        mixed = jnp.zeros((PART, D), jnp.float32)
        tangent = jnp.zeros((PART, D), jnp.float32)
        for dy in range(QB):
            held = mine.at[rows, :] if dy == 0 else opart.at[quarter, group(dy), :]
            one = held[:, 0:D].astype(jnp.float32)
            two = held[:, D:].astype(jnp.float32)
            mixed = mixed + table[:, dy:dy + 1] * one
            tangent = tangent + (table[:, dy:dy + 1] * two + table[:, 4 + dy:5 + dy] * one)
        obuf[rows, 0:D] = mixed.astype(jnp.bfloat16)
        obuf[rows, D:] = tangent.astype(jnp.bfloat16)

        def f_start(i):
            @pl.when(i < OWN)
            def _():
                f_copy(i).start()

        loop(quarter * SLOTS, (quarter + 1) * SLOTS, f_start)

    def q_arrived(quarter):
        arrived(qoth.at[quarter], q_recv.at[quarter])

    def o_start(quarter):
        for dy in (2, 1, 3):
            o_copy(quarter, dy).start()
            st_copy(quarter, dy).start()

    def other_score(quarter, side):
        return score(qoth[quarter], othcol[quarter], side)

    def other_mix(quarter, side, held):
        mix(part.at[quarter], pstat.at[pl.ds(quarter * 2, 2)], side, *held)
        o_start(quarter)

    kept = score(qown[...], owncol[...], 2)
    q_arrived(0)
    held = other_score(0, 0)
    v_second_arrived()

    def step(i, held):
        q_arrived(i + 1)
        other_mix(i, i % 2, held)
        return other_score(i + 1, (i + 1) % 2)

    held = lax.fori_loop(0, 3, step, held)
    mix(mine, mstat, 2, *kept)
    other_mix(3, 1, held)
    loop(0, 4, merge)

    def waits(i):
        zk(i).wait_send()
        zv(i).wait_send()
        zq(i).wait_send()

    loop(0, OWN, waits)
    arrived(pbuf.at[0:OWN], zp_send)
    arrived(kpos.at[0:7], kp_send)
    arrived(qpos.at[0:3], qp_send)
    k_left()
    v_left()
    arrived(qoth, q_send)
    arrived(part, o_send)
    arrived(ostat.at[0:12], st_send)

    def place(head, held):
        cols = pl.ds(pl.multiple_of(head * D, D), D)
        out_ref[:, cols] = held[:, 0:D].astype(jnp.float32)
        tan_ref[:, cols] = held[:, D:].astype(jnp.float32)

    place(z, obuf[OWN * ROWS:, :])

    def finish(i):
        place((z - offset(i) + NZ) % NZ, rbuf[i])

    arrived(rbuf.at[0:OWN], f_recv)
    loop(0, OWN, finish)
    arrived(rbuf.at[0:OWN], f_send)


def attend(*args):
    dma = pltpu.SemaphoreType.DMA
    bf16, f32, i32 = jnp.bfloat16, jnp.float32, jnp.int32
    return pl.pallas_call(
        kernel,
        out_shape=(pltpu.VMEM((ROWS, NZ * D), f32),) * 2,
        in_specs=[pl.BlockSpec(memory_space=pl.ANY)] * 7,
        out_specs=(pl.BlockSpec(memory_space=pltpu.VMEM),) * 2,
        scratch_shapes=[pltpu.VMEM((ROWS, NZ * D), bf16)] * 6 + [
            pltpu.SMEM((ROWS,), i32),
            dma((7,)),
            pltpu.VMEM((BLOCK, 2 * D), bf16),
            pltpu.VMEM((BLOCK, 2 * D), bf16),
            pltpu.VMEM((BLOCK, 2 * D), bf16),
            pltpu.VMEM((1, D), i32),
            pltpu.VMEM((KB, BLOCK, 2 * D), bf16),
            pltpu.VMEM((KB, BLOCK, 2 * D), bf16),
            pltpu.VMEM((BLOCK, 2 * D), bf16),
            pltpu.VMEM((4, OTHERS, 2 * D), bf16),
            pltpu.VMEM((NZ, 1, D), i32),
            pltpu.VMEM((KB, 1, BLOCK), i32),
            pltpu.VMEM((QB, 1, BLOCK), i32),
            pltpu.VMEM((BLOCK, D), i32),
            pltpu.VMEM((4, OTHERS, D), i32),
            pltpu.VMEM((BLOCK, KB * BLOCK), f32),
            pltpu.VMEM((3, BLOCK, KB * BLOCK), bf16),
            pltpu.VMEM((3, BLOCK, KB * BLOCK), bf16),
            pltpu.VMEM((BLOCK, 2 * D), bf16),
            pltpu.VMEM((2, 8, HALF), f32),
            pltpu.VMEM((4, OTHERS, 2 * D), bf16),
            pltpu.VMEM((8, 8, HALF), f32),
            pltpu.VMEM((4, OTHERS, 2 * D), bf16),
            pltpu.VMEM((4 * QB, 8, HALF), f32),
            pltpu.VMEM((BLOCK, 2 * D), bf16),
            pltpu.VMEM((NZ, ROWS, 2 * D), bf16),
        ] + [
            dma((NZ,)), dma((2,)), dma((NZ,)), dma((2,)), dma((NZ,)), dma((4,)), dma, dma,
            dma, dma((3,)), dma, dma((3,)), dma, dma((4,)), dma, dma, dma, dma,
            dma, dma((4,)), dma, dma((4,)), dma, dma,
        ],
        compiler_params=pltpu.CompilerParams(
            collective_id=0, has_side_effects=True, vmem_limit_bytes=62 * 2 ** 20),
    )(*args)


def local(*args):
    mixed, tangent = attend(*args)
    return mixed.astype(jnp.bfloat16), tangent.astype(jnp.bfloat16)


def solution(mesh):
    rows = P(("seq", "head"), None)
    return jax.shard_map(
        local,
        mesh=mesh,
        in_specs=(rows,) * 6 + (P(("seq", "head")),),
        out_specs=(rows, rows),
        check_vma=False,
    )
```

```python
import jax
import jax.numpy as jnp
from jax import lax
from jax.experimental import pallas as pl
from jax.experimental.pallas import tpu as pltpu
from jax.sharding import PartitionSpec as P

D = 128
NZ = 16
ROWS = 16
BLOCK = NZ * ROWS
HALF = BLOCK // 2
PART = BLOCK // 4
OTHERS = 3 * PART
SLOTS = NZ // 4
KB = 8
QB = 4
SCALE = D ** -0.5
LOG2E = 1.4426950408889634
NEG = -1e30
MESH = pl.DeviceIdType.MESH
DISTANCES = (2, 1, 3)
OWN = NZ - 1


def offset(slot):
    i = NZ - 1 - slot
    return ((i + 1) // 2) * (2 * (i % 2) - 1)


def loop(start, stop, body):
    def step(i, carry):
        body(i)
        return carry

    lax.fori_loop(start, stop, step, 0)


def dot_t(a, b):
    return lax.dot_general(a, b, (((1,), (1,)), ((), ())), preferred_element_type=jnp.float32)


def kernel(q_hbm, k_hbm, v_hbm, dq_hbm, dk_hbm, dv_hbm, pos_hbm,
           out_ref,
           q_ref, k_ref, v_ref, dq_ref, dk_ref, dv_ref, pos_ref, in_sem,
           kpack, vpack, qpack, prow, kbuf, vbuf, qown, qoth, pbuf, kpos, qpos, owncol, othcol,
           s_buf, p_buf, w_buf, mine, mstat, part, pstat, opart, ostat, obuf, rbuf,
           zk_send, zk_recv, zv_send, zv_recv, zq_send, zq_recv, zp_send, zp_recv,
           k_send, k_recv, v_send, v_recv, q_send, q_recv,
           kp_send, kp_recv, qp_send, qp_recv,
           o_send, o_recv, st_send, st_recv, f_send, f_recv):
    s = lax.axis_index("seq")
    h = lax.axis_index("head")
    c = s % 2
    z = (s // 2) % NZ
    y = (h % 2) * 2 + s // (2 * NZ)
    x = h // 2

    def device(x_, y_, z_, c_):
        return (((y_ % 2) * NZ + z_) * 2 + c_, x_ * 2 + y_ // 2)

    def along_z(by):
        return device(x, y, (z + by + NZ) % NZ, c)

    def along_x(by):
        return device((x + by) % 4, y, z, c)

    def across_x(by):
        return device((x + by) % 4, y, z, 1 - c)

    def along_y(by):
        return device(x, (y + by) % 4, z, c)

    twin = device(x, y, z, 1 - c)

    def send(source, target, send_sem, recv_sem, to):
        return pltpu.make_async_remote_copy(
            source, target, send_sem, recv_sem, device_id=to, device_id_type=MESH)

    fetches = [
        pltpu.make_async_copy(source, held, in_sem.at[i])
        for i, (source, held) in enumerate((
            (k_hbm, k_ref), (dk_hbm, dk_ref), (pos_hbm, pos_ref), (v_hbm, v_ref), (dv_hbm, dv_ref),
            (dq_hbm, dq_ref), (q_hbm, q_ref)))
    ]
    for fetch in fetches:
        fetch.start()

    barrier = pltpu.get_barrier_semaphore()

    def greet(to):
        pl.semaphore_signal(barrier, inc=1, device_id=to, device_id_type=MESH)

    loop(0, OWN, lambda i: greet(along_z(offset(i))))
    for by in (1, 2, 3):
        greet(along_x(by))
        greet(across_x(by))
        greet(along_y(by))
    greet(twin)

    own = pl.ds(pl.multiple_of(z * ROWS, ROWS), ROWS)

    def pack(left, right, packed, place):
        for head in range(NZ):
            rows = pl.ds(head * ROWS, ROWS)
            cols = pl.ds(head * D, D)
            packed[rows, 0:D] = left[:, cols]
            packed[rows, D:] = right[:, cols]
        place[...] = packed[own, :]

    for fetch in fetches[:3]:
        fetch.wait()
    pack(k_ref, dk_ref, kpack, kbuf.at[0, OWN * ROWS:, :])
    lane = lax.broadcasted_iota(jnp.int32, (1, D), 1)
    row = jnp.zeros((1, D), jnp.int32)
    for i in range(ROWS):
        row = jnp.where(lane % ROWS == i, pos_ref[i], row)
    prow[...] = row
    pbuf[OWN] = row

    pl.semaphore_wait(barrier, NZ - 1 + 10)

    def arrived(ref, sem):
        pltpu.make_async_copy(ref, ref, sem).wait()

    def z_copy(packed, buf, send_sem, recv_sem, i):
        by = offset(i)
        source = pl.ds(pl.multiple_of(((z - by + NZ) % NZ) * ROWS, ROWS), ROWS)
        slot = pl.ds(pl.multiple_of(i * ROWS, ROWS), ROWS)
        target = buf.at[slot, :] if buf is qown else buf.at[0, slot, :]
        shared = i // SLOTS if buf is qown else i // (NZ // 2)
        return send(packed.at[source, :], target, send_sem.at[i], recv_sem.at[shared], along_z(-by))

    def zk(i):
        return z_copy(kpack, kbuf, zk_send, zk_recv, i)

    def zv(i):
        return z_copy(vpack, vbuf, zv_send, zv_recv, i)

    def zq(i):
        return z_copy(qpack, qown, zq_send, zq_recv, i)

    def zp(i):
        return send(prow, pbuf.at[i], zp_send, zp_recv, along_z(-offset(i)))

    def gather(buf, send_sem, recv_sem):
        def copy(block, rows, to, at, sem):
            return send(buf.at[block, rows, :], buf.at[at, rows, :], send_sem, recv_sem.at[sem], to)

        def first(half):
            rows = pl.ds(half * HALF, HALF)
            return [
                copy(0, rows, along_x(2), 4, half),
                copy(0, rows, along_x(1), 6, half),
                copy(0, rows, along_x(3), 2, half),
                copy(0, rows, twin, 1, 2),
            ]

        def first_arrived(half):
            arrived(buf.at[0:3, half * HALF:(half + 1) * HALF, :], recv_sem.at[half])

        def second(half):
            rows = pl.ds(half * HALF, HALF)
            return [copy(block, rows, twin, block + 1, 2) for block in (2, 6, 4)]

        def second_arrived():
            arrived(buf.at[0:4], recv_sem.at[2])

        def left():
            arrived(buf.at[0:7], send_sem)

        return first, first_arrived, second, second_arrived, left

    k_first, k_first_arrived, k_second, k_second_arrived, k_left = gather(kbuf, k_send, k_recv)
    v_first, v_first_arrived, v_second, v_second_arrived, v_left = gather(vbuf, v_send, v_recv)

    def group(dy):
        return pl.ds(DISTANCES.index(dy) * PART, PART)

    def q_copy(quarter, dy):
        return send(qown.at[quarter * PART:(quarter + 1) * PART, :], qoth.at[quarter, group(dy), :],
                    q_send, q_recv.at[quarter], along_y(4 - dy))

    def q_copies(quarter):
        return [q_copy(quarter, dy) for dy in (2, 1, 3)]

    def kp_copy(to, at):
        return send(kpos.at[0], kpos.at[at], kp_send, kp_recv, to)

    def qp_copy(to, at):
        return send(kpos.at[0], qpos.at[at], qp_send, qp_recv, to)

    def pos_copies():
        copies = [kp_copy(twin, 1)]
        for by in (1, 2, 3):
            copies.append(kp_copy(along_x(4 - by), 2 * by))
            copies.append(kp_copy(across_x(4 - by), 2 * by + 1))
            copies.append(qp_copy(along_y(4 - by), by))
        return copies

    def start_all(copies):
        for copy in copies:
            copy.start()

    def first_z(i):
        zk(i).start()
        zp(i).start()

    loop(0, OWN, first_z)
    for fetch in fetches[3:5]:
        fetch.wait()
    pack(v_ref, dv_ref, vpack, vbuf.at[0, OWN * ROWS:, :])

    loop(0, OWN, lambda i: zv(i).start())
    for fetch in fetches[5:]:
        fetch.wait()
    pack(dq_ref, q_ref, qpack, qown.at[OWN * ROWS:, :])
    loop(0, OWN, lambda i: zq(i).start())
    arrived(kbuf.at[0, 0:HALF, :], zk_recv.at[0])
    start_all(k_first(0))
    arrived(pbuf.at[0:OWN], zp_recv)
    total = []
    for g in range(2):
        line = jnp.zeros((1, D), jnp.int32)
        for i in range(8):
            line = jnp.where(lane // ROWS == i, pbuf[g * 8 + i], line)
        total.append(line)
    line = jnp.concatenate(total, axis=1)
    kpos[0] = line
    qpos[0] = line
    start_all(pos_copies())
    arrived(kbuf.at[0, HALF:OWN * ROWS, :], zk_recv.at[1])
    start_all(k_first(1))
    k_first_arrived(0)
    start_all(k_second(0))
    arrived(vbuf.at[0, 0:HALF, :], zv_recv.at[0])
    start_all(v_first(0))
    arrived(vbuf.at[0, HALF:OWN * ROWS, :], zv_recv.at[1])
    start_all(v_first(1))
    k_first_arrived(1)
    start_all(k_second(1))
    arrived(kpos.at[0:7], kp_recv)
    arrived(qpos.at[0:3], qp_recv)
    for dy in range(QB):
        for half in range(2):
            line = qpos[dy, :, half * HALF:(half + 1) * HALF]
            line = jnp.transpose(jnp.broadcast_to(line, (HALF, HALF)))
            if dy == 0:
                owncol[half * HALF:(half + 1) * HALF, :] = line
            else:
                othcol[2 * half, group(dy), :] = line[0:PART]
                othcol[2 * half + 1, group(dy), :] = line[PART:]
    for quarter in range(4):
        rows = PART if quarter < 3 else PART - ROWS
        arrived(qown.at[quarter * PART:quarter * PART + rows, :], zq_recv.at[quarter])
        start_all(q_copies(quarter))
        if quarter == 0:
            v_first_arrived(0)
            start_all(v_second(0))
    v_first_arrived(1)
    start_all(v_second(1))
    k_second_arrived()

    def score(queries, places, side):
        rows = queries.shape[0]
        top = jnp.full((rows, D), NEG, jnp.float32)
        for b in range(KB):
            scores = dot_t(queries[:, D:], kbuf[b, :, 0:D])
            for at in range(0, BLOCK, D):
                seen = jnp.where(kpos[b, :, at:at + D] <= places, scores[:, at:at + D], NEG)
                s_buf[0:rows, b * BLOCK + at:b * BLOCK + at + D] = seen
                top = jnp.maximum(top, seen)
        top = jnp.max(top, axis=1, keepdims=True)
        total = jnp.zeros((rows, D), jnp.float32)
        for b in range(KB):
            cols = pl.ds(b * BLOCK, BLOCK)
            expo = jnp.exp2((s_buf[0:rows, cols] - top) * (SCALE * LOG2E))
            weighted = expo * dot_t(queries, kbuf[b])
            total = total + (expo[:, :D] + expo[:, D:])
            p_buf[side, 0:rows, cols] = expo.astype(jnp.bfloat16)
            w_buf[side, 0:rows, cols] = weighted.astype(jnp.bfloat16)
        return top, jnp.sum(total, axis=1, keepdims=True)

    def mix(held, stats_held, side, top, total):
        rows = held.shape[0]
        both = jnp.zeros((rows, 2 * D), jnp.float32)
        third = jnp.zeros((rows, 2 * D), jnp.float32)
        ones = jnp.ones((BLOCK, D), jnp.bfloat16)
        for b in range(KB):
            cols = pl.ds(b * BLOCK, BLOCK)
            both = both + jnp.dot(p_buf[side, 0:rows, cols], vbuf[b], preferred_element_type=jnp.float32)
            third = third + jnp.dot(
                w_buf[side, 0:rows, cols], jnp.concatenate([vbuf[b, :, 0:D], ones], axis=1),
                preferred_element_type=jnp.float32)
        inverse = 1.0 / total
        mean = third[:, D:] * (SCALE * inverse)
        mixed = both[:, :D] * inverse
        tangent = (third[:, :D] * SCALE + both[:, D:]) * inverse - mean * mixed
        lanes = lax.broadcasted_iota(jnp.int32, (rows, D), 1)
        stats = jnp.where(lanes == 0, top * (SCALE * LOG2E), jnp.where(lanes == 1, total, mean))
        held[:, 0:D] = mixed.astype(jnp.bfloat16)
        held[:, D:] = tangent.astype(jnp.bfloat16)
        stats_held[0] = jnp.transpose(stats[0:D])[0:8]
        rest = stats[D:]
        if rows < BLOCK:
            rest = jnp.concatenate([rest, rest], axis=0)
        stats_held[1] = jnp.transpose(rest)[0:8]

    def o_copy(quarter, dy):
        return send(part.at[quarter, group(dy), :], opart.at[quarter, group(dy), :],
                    o_send, o_recv.at[quarter], along_y(dy))

    def st_copy(quarter, dy):
        return send(pstat.at[quarter * 2 + DISTANCES.index(dy) // 2], ostat.at[quarter * 4 + dy],
                    st_send, st_recv.at[quarter], along_y(dy))

    def f_copy(i):
        slot = pl.ds(pl.multiple_of(i * ROWS, ROWS), ROWS)
        return send(obuf.at[slot, :], rbuf.at[i], f_send, f_recv, along_z(offset(i)))

    def merge(quarter):
        arrived(part.at[quarter], o_recv.at[quarter])
        arrived(pstat.at[0:3], st_recv.at[quarter])
        line = mstat[quarter // 2]
        lines = [jnp.where(quarter % 2 == 1, pltpu.roll(line, PART, 1), line)]
        for dy in (1, 2, 3):
            line = ostat[quarter * 4 + dy]
            lines.append(pltpu.roll(line, PART, 1) if DISTANCES.index(dy) % 2 else line)
        tops = [line[0:1] for line in lines]
        top = jnp.maximum(jnp.maximum(tops[0], tops[1]), jnp.maximum(tops[2], tops[3]))
        shares = [line[1:2] * jnp.exp2(line[0:1] - top) for line in lines]
        inverse = 1.0 / (shares[0] + shares[1] + shares[2] + shares[3])
        shares = [share * inverse for share in shares]
        mean = sum(share * line[2:3] for share, line in zip(shares, lines))
        shifts = [share * (line[2:3] - mean) for share, line in zip(shares, lines)]
        table = jnp.concatenate(shares + shifts + [jnp.zeros((D - 8, HALF), jnp.float32)], axis=0)
        table = jnp.transpose(table)
        table = table[0:PART]
        rows = pl.ds(pl.multiple_of(quarter * PART, PART), PART)
        mixed = jnp.zeros((PART, D), jnp.float32)
        tangent = jnp.zeros((PART, D), jnp.float32)
        for dy in range(QB):
            held = mine.at[rows, :] if dy == 0 else opart.at[quarter, group(dy), :]
            one = held[:, 0:D].astype(jnp.float32)
            two = held[:, D:].astype(jnp.float32)
            mixed = mixed + table[:, dy:dy + 1] * one
            tangent = tangent + (table[:, dy:dy + 1] * two + table[:, 4 + dy:5 + dy] * one)
        obuf[rows, 0:D] = mixed.astype(jnp.bfloat16)
        obuf[rows, D:] = tangent.astype(jnp.bfloat16)

        def f_start(i):
            @pl.when(i < OWN)
            def _():
                f_copy(i).start()

        loop(quarter * SLOTS, (quarter + 1) * SLOTS, f_start)

    def q_arrived(quarter):
        arrived(qoth.at[quarter], q_recv.at[quarter])

    def o_start(quarter):
        for dy in (2, 1, 3):
            o_copy(quarter, dy).start()
            st_copy(quarter, dy).start()

    def other_score(quarter, side):
        return score(qoth[quarter], othcol[quarter], side)

    def other_mix(quarter, side, held):
        mix(part.at[quarter], pstat.at[pl.ds(quarter * 2, 2)], side, *held)
        o_start(quarter)

    kept = score(qown[...], owncol[...], 2)
    q_arrived(0)
    held = other_score(0, 0)
    v_second_arrived()

    def step(i, held):
        q_arrived(i + 1)
        other_mix(i, i % 2, held)
        return other_score(i + 1, (i + 1) % 2)

    held = lax.fori_loop(0, 3, step, held)
    mix(mine, mstat, 2, *kept)
    other_mix(3, 1, held)
    loop(0, 4, merge)

    def waits(i):
        zk(i).wait_send()
        zv(i).wait_send()
        zq(i).wait_send()

    loop(0, OWN, waits)
    arrived(pbuf.at[0:OWN], zp_send)
    arrived(kpos.at[0:7], kp_send)
    arrived(qpos.at[0:3], qp_send)
    k_left()
    v_left()
    arrived(qoth, q_send)
    arrived(part, o_send)
    arrived(ostat.at[0:12], st_send)

    def place(head, held):
        cols = pl.ds(pl.multiple_of(head * D, D), D)
        out_ref[0, :, cols] = held[:, 0:D]
        out_ref[1, :, cols] = held[:, D:]

    place(z, obuf[OWN * ROWS:, :])

    def finish(i):
        place((z - offset(i) + NZ) % NZ, rbuf[i])

    arrived(rbuf.at[0:OWN], f_recv)
    loop(0, OWN, finish)
    arrived(rbuf.at[0:OWN], f_send)


def attend(*args):
    dma = pltpu.SemaphoreType.DMA
    bf16, f32, i32 = jnp.bfloat16, jnp.float32, jnp.int32
    return pl.pallas_call(
        kernel,
        out_shape=pltpu.VMEM((2, ROWS, NZ * D), bf16),
        in_specs=[pl.BlockSpec(memory_space=pl.ANY)] * 7,
        out_specs=pl.BlockSpec(memory_space=pltpu.VMEM),
        scratch_shapes=[pltpu.VMEM((ROWS, NZ * D), bf16)] * 6 + [
            pltpu.SMEM((ROWS,), i32),
            dma((7,)),
            pltpu.VMEM((BLOCK, 2 * D), bf16),
            pltpu.VMEM((BLOCK, 2 * D), bf16),
            pltpu.VMEM((BLOCK, 2 * D), bf16),
            pltpu.VMEM((1, D), i32),
            pltpu.VMEM((KB, BLOCK, 2 * D), bf16),
            pltpu.VMEM((KB, BLOCK, 2 * D), bf16),
            pltpu.VMEM((BLOCK, 2 * D), bf16),
            pltpu.VMEM((4, OTHERS, 2 * D), bf16),
            pltpu.VMEM((NZ, 1, D), i32),
            pltpu.VMEM((KB, 1, BLOCK), i32),
            pltpu.VMEM((QB, 1, BLOCK), i32),
            pltpu.VMEM((BLOCK, D), i32),
            pltpu.VMEM((4, OTHERS, D), i32),
            pltpu.VMEM((BLOCK, KB * BLOCK), f32),
            pltpu.VMEM((3, BLOCK, KB * BLOCK), bf16),
            pltpu.VMEM((3, BLOCK, KB * BLOCK), bf16),
            pltpu.VMEM((BLOCK, 2 * D), bf16),
            pltpu.VMEM((2, 8, HALF), f32),
            pltpu.VMEM((4, OTHERS, 2 * D), bf16),
            pltpu.VMEM((8, 8, HALF), f32),
            pltpu.VMEM((4, OTHERS, 2 * D), bf16),
            pltpu.VMEM((4 * QB, 8, HALF), f32),
            pltpu.VMEM((BLOCK, 2 * D), bf16),
            pltpu.VMEM((NZ, ROWS, 2 * D), bf16),
        ] + [
            dma((NZ,)), dma((2,)), dma((NZ,)), dma((2,)), dma((NZ,)), dma((4,)), dma, dma,
            dma, dma((3,)), dma, dma((3,)), dma, dma((4,)), dma, dma, dma, dma,
            dma, dma((4,)), dma, dma((4,)), dma, dma,
        ],
        compiler_params=pltpu.CompilerParams(
            collective_id=0, has_side_effects=True, vmem_limit_bytes=62 * 2 ** 20),
    )(*args)


def local(*args):
    both = attend(*args)
    return both[0], both[1]


def solution(mesh):
    rows = P(("seq", "head"), None)
    return jax.shard_map(
        local,
        mesh=mesh,
        in_specs=(rows,) * 6 + (P(("seq", "head")),),
        out_specs=(rows, rows),
        check_vma=False,
    )
```
